256 devices in a mesh: section: 8 (over y, core), outer: 8 (over z_lo, x), inner: 4 (over z_hi).
Axes of the slice: x: 4, y: 4, z: 8 (z_hi: 4, z_lo: 2; z = z_hi * 2 + z_lo), core: 2. Of those that a mesh axis runs over, the one named last changes fastest.
Arguments:
- projected: bfloat16 [8, 4096, 1280], P('section', ('outer', 'inner')), may hold values from -64 to 64
- positions: int32 [4096], replicated, may hold values from 0 to 4095, as said below
- out_weight: bfloat16 [8, 1024, 16384], P('section', None, ('outer', 'inner')), may hold values from -1.5 to 1.5
- residual: bfloat16 [8, 4096, 16384], P('section', None, ('outer', 'inner')), may hold values from -8 to 8
- norm_gain: bfloat16 [8, 16384], P('section', ('outer', 'inner')), may hold values from 0.099609375 to 1.8984375
- next_weight: bfloat16 [8, 16384, 1280], P('section', ('outer', 'inner')), may hold values from -0.046875 to 0.046875
Outputs:
- next_projected: bfloat16 [8, 4096, 1280], P('section', ('outer', 'inner'))
- stream: bfloat16 [8, 4096, 16384], P('section', None, ('outer', 'inner'))
The draws below stay inside these ranges and needn't reach their ends.
Inputs may be any that keep to these rules, and one draw needn't show every extreme that they name: Each aligned run of 64 stored tokens holds consecutive positions starting at a multiple of 64; every position 0 to 4095 is stored once.
All inputs are finite; a program needn't handle non-finite values.
Results may differ from the reference program's by a relative error of at most 0.023.
Values may be sent and summed in bfloat16 or wider, within the bound.
No kernel may reach another device: no remote copies, remote signals or barrier semaphores. Data moves between devices by JAX's collectives and lax.ppermute only.
A program may use at most 128 MiB of HBM per device.

```python
import jax
import jax.numpy as jnp
from jax import lax

D = 16384
HQ = 8
HD = 128
TOK_DEV = 128
SECTIONS = 8
SEQ = 4096
QW = 1280
N_OUTER = 8
N_INNER = 4


def draw_projected(key, part):
    shape = (SECTIONS, SEQ, QW)
    result = jax.random.truncated_normal(key, -6.0, 6.0, shape, jnp.float32)
    return result.astype(jnp.bfloat16)


def draw_positions(key, part):
    span_count = 2 * N_OUTER * N_INNER
    half_shard = TOK_DEV // 2
    order = jax.random.permutation(key, span_count).astype(jnp.int32)
    rows_index = jnp.arange(SEQ, dtype=jnp.int32)
    return (order[rows_index // half_shard] * half_shard + rows_index % half_shard).astype(jnp.int32)


def draw_residual(key, part):
    shape = (SECTIONS, SEQ, D)
    first, second = jax.random.split(key)
    column_scale = 10.0 ** (jnp.arange(D, dtype=jnp.float32) / D)
    row_scale = 10.0 ** jax.random.uniform(second, (SECTIONS, SEQ, 1), jnp.float32, 0.0, 1.0)
    noise = jax.random.truncated_normal(first, -6.0, 6.0, shape, jnp.float32)
    return (0.012 * noise * row_scale * column_scale[None, None, :]).astype(jnp.bfloat16)


def block_scale(own_key, dims, pieces, low, high):
    level = 1.0
    for position, blocks in pieces:
        heights = jax.random.uniform(jax.random.fold_in(jax.random.fold_in(own_key, 6), position), (blocks,), jnp.float32, low / len(pieces), high / len(pieces))
        level = level * jnp.repeat(jnp.exp(heights), dims[position] // blocks).reshape((-1,) + (1,) * (len(dims) - 1 - position))
    return level


def gaussian(own_key, shape, width, bound, cuts=(), kind=jnp.bfloat16):
    drawn = jax.random.normal(own_key, shape, jnp.float32) * width
    if len(cuts) > 0:
        drawn = block_scale(own_key, shape, cuts, -0.22, 0.18) * drawn
    return jnp.clip(drawn, min=-bound, max=bound).astype(kind)


def setup_inputs(seed: int = 0) -> dict:
    splits = jax.random.split(jax.random.key(seed), 7)
    projected = draw_projected(jax.random.fold_in(splits[6], 71), 0)
    positions = draw_positions(jax.random.fold_in(splits[6], 71), 0)
    out_weight = gaussian(splits[2], (SECTIONS, HQ * HD, D), (3.0 / (HQ * HD) ** 0.5), 1.5, ((0, 8), (2, 32)))
    residual = draw_residual(jax.random.fold_in(splits[6], 71), 0)
    norm_gain = jnp.clip(1.0 + 0.18 * jax.random.normal(splits[4], (SECTIONS, D), jnp.float32), 0.099609375, 1.8984375).astype(jnp.bfloat16)
    next_weight = gaussian(splits[5], (SECTIONS, D, QW), D ** -0.5, 0.046875, ((0, 8), (1, 32)))
    return {"projected": projected, "positions": positions, "out_weight": out_weight, "residual": residual, "norm_gain": norm_gain, "next_weight": next_weight}


def attend_block(query_block, block_positions, keys, values, positions):
    scores = jnp.einsum('thd,jd->htj', query_block.astype(jnp.float32), keys.astype(jnp.float32)) * HD ** (-0.5)
    visible = positions[None, None, :] <= block_positions[None, :, None]
    scores = jnp.where(visible, scores, -jnp.inf)
    largest = lax.optimization_barrier(jnp.max(scores, axis=-1, keepdims=True))
    weights = jnp.where(visible, jnp.exp(scores - largest), 0.0)
    totals = lax.optimization_barrier(jnp.sum(weights, axis=-1))
    rounded = lax.optimization_barrier(weights.astype(jnp.bfloat16)).astype(jnp.float32)
    mixed = jnp.einsum('htj,jd->htd', rounded, values.astype(jnp.float32)) / totals[..., None]
    return jnp.transpose(mixed, (1, 0, 2)).reshape(-1, HQ * HD).astype(jnp.bfloat16)

def reference(projected, positions, out_weight, residual, norm_gain, next_weight):
    shard_count = N_OUTER * N_INNER

    def section_out(inputs):
        token_rows, weight_out, residual_rows = inputs
        queries = token_rows[:, :HQ * HD].reshape(shard_count, TOK_DEV, HQ, HD)
        keys = token_rows[:, HQ * HD:HQ * HD + HD]
        values = token_rows[:, HQ * HD + HD:]
        block_positions = positions.reshape(shard_count, TOK_DEV)
        attended = lax.map(lambda pair: attend_block(pair[0], pair[1], keys, values, positions), (queries, block_positions))
        attended = attended.reshape(SEQ, HQ * HD)
        product = jnp.dot(attended, weight_out, preferred_element_type=jnp.float32)
        return (residual_rows.astype(jnp.float32) + product).astype(jnp.bfloat16)
    hidden = lax.map(section_out, (projected, out_weight, residual))
    stream = jnp.roll(hidden, 1, axis=0)
    block_width = D // shard_count

    def section_in(inputs):
        stream_rows, gain, weight_next = inputs
        values32 = stream_rows.astype(jnp.float32)
        inverse_rms = lax.rsqrt(lax.optimization_barrier(jnp.mean(values32 * values32, axis=1)) + 1e-05)
        normed = (values32 * inverse_rms[:, None] * gain.astype(jnp.float32)[None, :]).astype(jnp.bfloat16)
        normed_blocks = jnp.transpose(normed.reshape(SEQ, shard_count, block_width), (1, 0, 2))
        weight_blocks = weight_next.reshape(shard_count, block_width, QW)

        def add_block(total, block_pair):
            partial_sum = jnp.dot(block_pair[0], block_pair[1], preferred_element_type=jnp.float32)
            partial_sum = lax.optimization_barrier(partial_sum.astype(jnp.bfloat16)).astype(jnp.float32)
            return (total + partial_sum, None)
        total, unused = lax.scan(add_block, jnp.zeros((SEQ, QW), jnp.float32), (normed_blocks, weight_blocks))
        return total.astype(jnp.bfloat16)
    next_projected = lax.map(section_in, (stream, norm_gain, next_weight))
    return (next_projected, stream)
```

```python
import functools

import jax
import jax.numpy as jnp
from jax import lax
from jax.experimental import pallas as pl
from jax.experimental.pallas import tpu as pltpu
from jax.sharding import PartitionSpec as P

D = 16384
HQ = 8
HD = 128
QW = 1280
SUB = 64
PW = QW + 128
NX = 4
NZ = 8
SHARD_AXES = ("outer", "inner")
Z_ORDER = (0, 4, -1, 3, 1, -3, -2, 2)
X_ORDER = (0, -1, 1, 2)


def shard_of(x, z):
    x = x % NX
    z = z % NZ
    return (z % 2) * 16 + x * 4 + z // 2


def shift(value, dx, dz):
    pairs = [
        (shard_of(x, z), shard_of(x + dx, z + dz)) for x in range(NX) for z in range(NZ)
    ]
    return lax.ppermute(value, SHARD_AXES, pairs)


def section_shift(value, by):
    return lax.ppermute(value, "section", [(i, (i + by) % 8) for i in range(8)])


def gather(value):
    chunks = {}
    first = value[:SUB]
    second = value[SUB:]
    row = jnp.concatenate(
        [second, shift(second, 1, 0), shift(second, -1, 0), shift(second, 2, 0)], axis=0
    )
    opposite = shift(first, 0, 4)
    pair = jnp.concatenate([first, opposite], axis=0)
    up = shift(pair, 0, 1)
    down = shift(pair, 0, -1)
    chunks["row"] = (row, [(1, dx, 0) for dx in X_ORDER])
    up1 = shift(row, 0, 1)
    down1 = shift(row, 0, -1)
    chunks["up1"] = (up1, [(1, dx, -1) for dx in X_ORDER])
    chunks["down1"] = (down1, [(1, dx, 1) for dx in X_ORDER])
    up_far = shift(up[:SUB], 0, 1)
    down_far = shift(down[:SUB], 0, -1)
    col = jnp.concatenate([pair, up, down, up_far, down_far], axis=0)
    chunks["col"] = (col, [(0, 0, dz) for dz in Z_ORDER])
    head, tail = col[: 4 * SUB], col[4 * SUB :]
    left_head = shift(head, 1, 0)
    right_tail = shift(tail, -1, 0)
    left_tail = shift(tail, 1, 0)
    right_head = shift(head, -1, 0)
    up2 = shift(up1, 0, 1)
    down2 = shift(down1, 0, -1)
    chunks["up2"] = (up2, [(1, dx, -2) for dx in X_ORDER])
    chunks["down2"] = (down2, [(1, dx, 2) for dx in X_ORDER])
    far_head = shift(left_head, 1, 0)
    far_tail = shift(right_tail, -1, 0)
    chunks["left_head"] = (left_head, [(0, -1, dz) for dz in Z_ORDER[:4]])
    chunks["left_tail"] = (left_tail, [(0, -1, dz) for dz in Z_ORDER[4:]])
    chunks["right_head"] = (right_head, [(0, 1, dz) for dz in Z_ORDER[:4]])
    chunks["right_tail"] = (right_tail, [(0, 1, dz) for dz in Z_ORDER[4:]])
    up3 = shift(up2, 0, 1)
    down3 = shift(down2, 0, -1)
    chunks["up3"] = (up3, [(1, dx, -3) for dx in X_ORDER])
    chunks["down3"] = (down3, [(1, dx, 3) for dx in X_ORDER])
    chunks["far_head"] = (far_head, [(0, 2, dz) for dz in Z_ORDER[:4]])
    chunks["far_tail"] = (far_tail, [(0, 2, dz) for dz in Z_ORDER[4:]])
    up4 = shift(up3[: 2 * SUB], 0, 1)
    down4 = shift(down3[2 * SUB :], 0, -1)
    chunks["up4"] = (up4, [(1, dx, 4) for dx in X_ORDER[:2]])
    chunks["down4"] = (down4, [(1, dx, 4) for dx in X_ORDER[2:]])
    return chunks


def add(*terms):
    total = terms[0].astype(jnp.float32)
    for term in terms[1:]:
        total = total + term.astype(jnp.float32)
    return total.astype(jnp.bfloat16)


def reduce_scatter(part):
    to_right = shift(part["far_head"], 1, 0)
    to_left = shift(part["far_tail"], -1, 0)
    from_left_tail = shift(part["right_tail"], 1, 0)
    from_right_head = shift(part["left_head"], -1, 0)
    top = shift(part["up4"], 0, -1)
    bottom = shift(part["down4"], 0, 1)
    up3 = jnp.concatenate([add(part["up3"][: 2 * SUB], top), part["up3"][2 * SUB :]], axis=0)
    down3 = jnp.concatenate(
        [part["down3"][: 2 * SUB], add(part["down3"][2 * SUB :], bottom)], axis=0
    )
    top = shift(up3, 0, -1)
    bottom = shift(down3, 0, 1)
    from_left_head = shift(add(part["right_head"], to_right), 1, 0)
    from_right_tail = shift(add(part["left_tail"], to_left), -1, 0)
    top = shift(add(part["up2"], top), 0, -1)
    bottom = shift(add(part["down2"], bottom), 0, 1)
    col_head = add(part["col"][: 4 * SUB], from_left_head, from_right_head)
    col_tail = add(part["col"][4 * SUB :], from_left_tail, from_right_tail)
    below = shift(col_tail[2 * SUB : 3 * SUB], 0, -1)
    above = shift(col_tail[3 * SUB :], 0, 1)
    top = shift(add(part["up1"], top), 0, -1)
    bottom = shift(add(part["down1"], bottom), 0, 1)
    pair_down = jnp.concatenate(
        [add(col_head[2 * SUB : 3 * SUB], below), col_head[3 * SUB :]], axis=0
    )
    pair_up = jnp.concatenate([add(col_tail[:SUB], above), col_tail[SUB : 2 * SUB]], axis=0)
    pair = add(col_head[: 2 * SUB], shift(pair_down, 0, -1), shift(pair_up, 0, 1))
    row = add(part["row"], top, bottom)
    first = pair[:SUB].astype(jnp.float32) + shift(pair[SUB:], 0, 4).astype(jnp.float32)
    second = (
        row[:SUB].astype(jnp.float32)
        + shift(row[SUB : 2 * SUB], -1, 0).astype(jnp.float32)
        + shift(row[2 * SUB : 3 * SUB], 1, 0).astype(jnp.float32)
        + shift(row[3 * SUB :], 2, 0).astype(jnp.float32)
    )
    return jnp.concatenate([first, second], axis=0)


def project_kernel(sizes, offsets, *refs):
    count = len(sizes)
    chunk_refs = refs[:count]
    weight_out, residual, gain, weight_next, _ = refs[count : count + 5]
    hidden = refs[count + 5]
    part_refs = refs[count + 6 : 2 * count + 6]
    rows_in, rows_out, in_sems, out_sems = refs[2 * count + 6 :]
    starts = [sum(sizes[:i]) for i in range(count)]

    def fetch(sub):
        offset = pl.multiple_of(offsets[sub], SUB)
        return pltpu.make_async_copy(
            residual.at[pl.ds(offset, SUB)], rows_in.at[pl.ds(sub * SUB, SUB)], in_sems.at[sub]
        )

    def store(sub):
        offset = pl.multiple_of(offsets[sub], SUB)
        return pltpu.make_async_copy(
            rows_out.at[pl.ds(sub * SUB, SUB)], hidden.at[pl.ds(offset, SUB)], out_sems.at[sub]
        )

    subs = sum(sizes) // SUB
    for sub in range(subs):
        fetch(sub).start()
    for chunk, size, start, part in zip(chunk_refs, sizes, starts, part_refs):
        product = jnp.dot(chunk[...], weight_out[...], preferred_element_type=jnp.float32)
        for sub in range(start // SUB, (start + size) // SUB):
            fetch(sub).wait()
        rows = (rows_in[pl.ds(start, size)].astype(jnp.float32) + product).astype(jnp.bfloat16)
        rows_out[pl.ds(start, size)] = rows
        for sub in range(start // SUB, (start + size) // SUB):
            store(sub).start()
        wide = rows.astype(jnp.float32)
        scaled = (wide * gain[...].astype(jnp.float32)).astype(jnp.bfloat16)
        part[:, :QW] = jnp.dot(
            scaled, weight_next[...], preferred_element_type=jnp.float32
        ).astype(jnp.bfloat16)
        squares = jnp.sum(wide * wide, axis=1, keepdims=True)
        part[:, QW:] = jnp.broadcast_to(squares, (size, PW - QW)).astype(jnp.bfloat16)
    for sub in range(subs):
        store(sub).wait()


def project(chunks, offsets, weight_out, residual, gain, weight_next, hidden):
    sizes = [chunk.shape[0] for chunk in chunks]
    total = sum(sizes)
    width = weight_out.shape[1]
    vmem = pl.BlockSpec(memory_space=pltpu.VMEM)
    anywhere = pl.BlockSpec(memory_space=pl.ANY)
    outs = pl.pallas_call(
        functools.partial(project_kernel, sizes),
        out_shape=[jax.ShapeDtypeStruct(hidden.shape, hidden.dtype)]
        + [jax.ShapeDtypeStruct((size, PW), jnp.bfloat16) for size in sizes],
        in_specs=[pl.BlockSpec(memory_space=pltpu.SMEM)]
        + [vmem] * len(sizes)
        + [vmem, anywhere, vmem, vmem, anywhere],
        out_specs=[anywhere] + [vmem] * len(sizes),
        scratch_shapes=[
            pltpu.VMEM((total, width), jnp.bfloat16),
            pltpu.VMEM((total, width), jnp.bfloat16),
            pltpu.SemaphoreType.DMA((total // SUB,)),
            pltpu.SemaphoreType.DMA((total // SUB,)),
        ],
        input_output_aliases={1 + len(sizes) + 4: 0},
        compiler_params=pltpu.CompilerParams(vmem_limit_bytes=40 * 1024 * 1024),
        cost_estimate=pl.CostEstimate(
            flops=2 * total * width * (HQ * HD + QW),
            bytes_accessed=2 * total * (HQ * HD + 2 * width + PW) + 2 * width * (HQ * HD + QW),
            transcendentals=0,
        ),
    )(offsets, *chunks, weight_out, residual, gain, weight_next, hidden)
    return outs[0], outs[1:]


GROUPS = (
    ("row", "up1", "down1"),
    ("col", "left_head", "right_tail", "up2", "down2"),
    ("left_tail", "right_head", "up3", "down3"),
    ("far_head", "far_tail", "up4", "down4"),
)


def body(projected, positions, out_weight, residual, norm_gain, next_weight):
    local_rows = projected[0]
    tokens_here = local_rows.shape[0]
    outer = lax.axis_index("outer")
    inner = lax.axis_index("inner")
    here_x = outer % NX
    here_z = inner * 2 + outer // NX

    def offset_of(half, dx, dz):
        return (shard_of(here_x + dx + NX, here_z + dz + NZ) * 2 + half) * SUB

    weight_next = section_shift(next_weight, -1)[0]
    gain = section_shift(norm_gain, -1)

    kv_chunks = gather(local_rows[:, HQ * HD :])
    key_value = jnp.concatenate([kv_chunks[name][0] for name in kv_chunks], axis=0)
    key_offsets = jnp.stack([offset_of(*run) for name in kv_chunks for run in kv_chunks[name][1]])
    key_positions = jnp.take(positions.reshape(-1, SUB), key_offsets // SUB, axis=0).reshape(-1)
    query_positions = lax.dynamic_slice_in_dim(
        positions, offset_of(0, 0, 0), tokens_here
    )
    queries = local_rows[:, : HQ * HD].reshape(tokens_here, HQ, HD)
    scale_factor = HD ** (-0.5)
    keys = key_value[:, :HD]
    values = key_value[:, HD:]
    scores = (
        jnp.einsum("thd,jd->htj", queries, keys, preferred_element_type=jnp.float32) * scale_factor
    )
    visible = key_positions[None, None, :] <= query_positions[None, :, None]
    masked = jnp.where(visible, scores, -1e30)
    largest = jnp.max(masked, axis=-1)
    weights = jnp.where(visible, jnp.exp(scores - largest[..., None]), 0.0)
    totals = jnp.sum(weights, axis=-1)
    mixed = jnp.einsum(
        "htj,jd->htd", weights.astype(jnp.bfloat16), values, preferred_element_type=jnp.float32
    )
    attended = jnp.transpose(mixed / totals[..., None], (1, 0, 2))
    attended = attended.reshape(tokens_here, HQ * HD).astype(jnp.bfloat16)

    chunks = gather(attended)
    hidden = jnp.zeros(residual.shape[1:], residual.dtype)
    part = {}
    for names in GROUPS:
        offsets = jnp.stack([offset_of(*run) for name in names for run in chunks[name][1]])
        hidden, parts = project(
            [chunks[name][0] for name in names],
            offsets,
            out_weight[0],
            residual[0],
            gain,
            weight_next,
            hidden,
        )
        part.update(zip(names, parts))
    stream = section_shift(hidden[None], 1)
    summed = reduce_scatter(part)
    inverse_rms = lax.rsqrt(summed[:, QW : QW + 1] / D + 1e-05)
    result = (summed[:, :QW] * inverse_rms).astype(jnp.bfloat16)
    return (section_shift(result[None], 1), stream)


def solution(mesh):
    return jax.shard_map(
        body,
        mesh=mesh,
        in_specs=(
            P("section", ("outer", "inner"), None),
            P(),
            P("section", None, ("outer", "inner")),
            P("section", None, ("outer", "inner")),
            P("section", ("outer", "inner")),
            P("section", ("outer", "inner"), None),
        ),
        out_specs=(P("section", ("outer", "inner"), None), P("section", None, ("outer", "inner"))),
        check_vma=False,
    )
```

```python
import functools

import jax
import jax.numpy as jnp
import numpy as np
from jax import lax
from jax.experimental import pallas as pl
from jax.experimental.pallas import tpu as pltpu
from jax.sharding import PartitionSpec as P

D = 16384
HQ = 8
HD = 128
QW = 1280
SUB = 64
PW = QW + 128
NX = 4
NZ = 8
SHARD_AXES = ("outer", "inner")
Z_ORDER = (0, 4, -1, 3, 1, -3, -2, 2)
X_ORDER = (0, -1, 1, 2)
KEY_BLOCK = 256


def shard_of(x, z):
    x = x & (NX - 1)
    z = z & (NZ - 1)
    return (z & 1) * 16 + x * 4 + (z >> 1)


def shift(value, dx, dz):
    pairs = [
        (shard_of(x, z), shard_of(x + dx, z + dz)) for x in range(NX) for z in range(NZ)
    ]
    return lax.ppermute(value, SHARD_AXES, pairs)


def section_shift(value, by):
    return lax.ppermute(value, "section", [(i, (i + by) % 8) for i in range(8)])


def gather(value):
    chunks = {}
    first = value[:SUB]
    second = value[SUB:]
    row = jnp.concatenate(
        [second, shift(second, 1, 0), shift(second, -1, 0), shift(second, 2, 0)], axis=0
    )
    opposite = shift(first, 0, 4)
    pair = jnp.concatenate([first, opposite], axis=0)
    up = shift(pair, 0, 1)
    down = shift(pair, 0, -1)
    chunks["row"] = (row, [(1, dx, 0) for dx in X_ORDER])
    up1 = shift(row, 0, 1)
    down1 = shift(row, 0, -1)
    chunks["up1"] = (up1, [(1, dx, -1) for dx in X_ORDER])
    chunks["down1"] = (down1, [(1, dx, 1) for dx in X_ORDER])
    up_far = shift(up[:SUB], 0, 1)
    down_far = shift(down[:SUB], 0, -1)
    col = jnp.concatenate([pair, up, down, up_far, down_far], axis=0)
    chunks["col"] = (col, [(0, 0, dz) for dz in Z_ORDER])
    head, tail = col[: 4 * SUB], col[4 * SUB :]
    left_head = shift(head, 1, 0)
    right_tail = shift(tail, -1, 0)
    left_tail = shift(tail, 1, 0)
    right_head = shift(head, -1, 0)
    up2 = shift(up1, 0, 1)
    down2 = shift(down1, 0, -1)
    chunks["up2"] = (up2, [(1, dx, -2) for dx in X_ORDER])
    chunks["down2"] = (down2, [(1, dx, 2) for dx in X_ORDER])
    far_head = shift(left_head, 1, 0)
    far_tail = shift(right_tail, -1, 0)
    chunks["left_head"] = (left_head, [(0, -1, dz) for dz in Z_ORDER[:4]])
    chunks["left_tail"] = (left_tail, [(0, -1, dz) for dz in Z_ORDER[4:]])
    chunks["right_head"] = (right_head, [(0, 1, dz) for dz in Z_ORDER[:4]])
    chunks["right_tail"] = (right_tail, [(0, 1, dz) for dz in Z_ORDER[4:]])
    up3 = shift(up2, 0, 1)
    down3 = shift(down2, 0, -1)
    chunks["up3"] = (up3, [(1, dx, -3) for dx in X_ORDER])
    chunks["down3"] = (down3, [(1, dx, 3) for dx in X_ORDER])
    chunks["far_head"] = (far_head, [(0, 2, dz) for dz in Z_ORDER[:4]])
    chunks["far_tail"] = (far_tail, [(0, 2, dz) for dz in Z_ORDER[4:]])
    up4 = shift(up3[: 2 * SUB], 0, 1)
    down4 = shift(down3[2 * SUB :], 0, -1)
    chunks["up4"] = (up4, [(1, dx, 4) for dx in X_ORDER[:2]])
    chunks["down4"] = (down4, [(1, dx, 4) for dx in X_ORDER[2:]])
    return chunks


def gather_rows(value):
    half = 2 * value.shape[0]
    left, right, far = shift(value, 1, 0), shift(value, -1, 0), shift(value, 2, 0)
    row = jnp.concatenate([value, left, right, far], axis=0)
    up1, down1 = shift(row, 0, 1), shift(row, 0, -1)
    up2, down2 = shift(up1, 0, 1), shift(down1, 0, -1)
    up3, down3 = shift(up2, 0, 1), shift(down2, 0, -1)
    up4, down4 = shift(up3[:half], 0, 1), shift(down3[half:], 0, -1)
    return (
        [(row, X_ORDER, 0)],
        [(up1, X_ORDER, -1), (down1, X_ORDER, 1)],
        [(up2, X_ORDER, -2), (down2, X_ORDER, 2)],
        [(up3, X_ORDER, -3), (down3, X_ORDER, 3)],
        [(up4, X_ORDER[:2], 4), (down4, X_ORDER[2:], 4)],
    )


def attend_kernel(sizes, is_first, is_last, key_starts, query_starts, *refs):
    count = len(sizes)
    queries = refs[0]
    chunks = refs[1 : count + 1]
    refs = refs[count + 1 :]
    tokens = queries.shape[0]
    columns = HQ * tokens
    if is_first:
        largest = jnp.full((1, columns), -1e30, jnp.float32)
        total = jnp.zeros((1, columns), jnp.float32)
        acc = jnp.zeros((HD, columns), jnp.float32)
    else:
        largest, total, acc = refs[0][...], refs[1][...], refs[2][...]
        refs = refs[3:]
    stacked = jnp.concatenate([queries[:, h * HD : (h + 1) * HD] for h in range(HQ)], axis=0)
    lane = lax.broadcasted_iota(jnp.int32, (1, tokens), 1)
    query_positions = lane
    for run in range(tokens // SUB):
        start = query_starts[run] - run * SUB
        query_positions = jnp.where(lane // SUB == run, lane + start, query_positions)
    row_index = lax.broadcasted_iota(jnp.int32, (SUB, tokens), 0)
    factor = HD ** (-0.5) * 1.4426950408889634
    run = 0
    for chunk, size in zip(chunks, sizes):
        for start in range(0, size, KEY_BLOCK):
            keys = chunk[pl.ds(start, KEY_BLOCK), :HD]
            values = chunk[pl.ds(start, KEY_BLOCK), HD:]
            scores = lax.dot_general(
                keys, stacked, (((1,), (1,)), ((), ())), preferred_element_type=jnp.float32
            )
            masked = []
            for part in range(KEY_BLOCK // SUB):
                visible = row_index + key_starts[run] <= query_positions
                visible = jnp.concatenate([visible] * HQ, axis=1)
                block = scores[part * SUB : (part + 1) * SUB] * factor
                masked.append(jnp.where(visible, block, -jnp.inf))
                run += 1
            masked = jnp.concatenate(masked, axis=0)
            new_largest = jnp.maximum(largest, jnp.max(masked, axis=0, keepdims=True))
            weights = jnp.exp2(masked - new_largest)
            keep = jnp.exp2(largest - new_largest)
            total = total * keep + jnp.sum(weights, axis=0, keepdims=True)
            acc = acc * keep + lax.dot_general(
                values,
                weights.astype(jnp.bfloat16),
                (((0,), (0,)), ((), ())),
                preferred_element_type=jnp.float32,
            )
            largest = new_largest
    if is_last:
        mixed = acc / total
        for h in range(HQ):
            refs[0][:, h * HD : (h + 1) * HD] = jnp.transpose(
                mixed[:, h * tokens : (h + 1) * tokens]
            ).astype(jnp.bfloat16)
    else:
        refs[0][...], refs[1][...], refs[2][...] = largest, total, acc


def attend(queries, chunks, key_starts, query_starts, state, is_last):
    sizes = [chunk.shape[0] for chunk in chunks]
    tokens = queries.shape[0]
    columns = HQ * tokens
    smem = pl.BlockSpec(memory_space=pltpu.SMEM)
    vmem = pl.BlockSpec(memory_space=pltpu.VMEM)
    if is_last:
        out_shape = [jax.ShapeDtypeStruct(queries.shape, jnp.bfloat16)]
    else:
        out_shape = [
            jax.ShapeDtypeStruct((1, columns), jnp.float32),
            jax.ShapeDtypeStruct((1, columns), jnp.float32),
            jax.ShapeDtypeStruct((HD, columns), jnp.float32),
        ]
    return pl.pallas_call(
        functools.partial(attend_kernel, sizes, not state, is_last),
        out_shape=out_shape,
        in_specs=[smem, smem] + [vmem] * (1 + len(chunks) + len(state)),
        out_specs=[vmem] * len(out_shape),
        compiler_params=pltpu.CompilerParams(vmem_limit_bytes=16 * 1024 * 1024),
        cost_estimate=pl.CostEstimate(
            flops=8 * sum(sizes) * columns * HD,
            bytes_accessed=4 * columns * HD,
            transcendentals=sum(sizes) * columns,
        ),
    )(key_starts, query_starts, queries, *chunks, *state)


def add(*terms):
    total = terms[0].astype(jnp.float32)
    for term in terms[1:]:
        total = total + term.astype(jnp.float32)
    return total.astype(jnp.bfloat16)


def reduce_scatter(part):
    to_right = shift(part["far_head"], 1, 0)
    to_left = shift(part["far_tail"], -1, 0)
    from_left_tail = shift(part["right_tail"], 1, 0)
    from_right_head = shift(part["left_head"], -1, 0)
    top = shift(part["up4"], 0, -1)
    bottom = shift(part["down4"], 0, 1)
    up3 = jnp.concatenate([add(part["up3"][: 2 * SUB], top), part["up3"][2 * SUB :]], axis=0)
    down3 = jnp.concatenate(
        [part["down3"][: 2 * SUB], add(part["down3"][2 * SUB :], bottom)], axis=0
    )
    top = shift(up3, 0, -1)
    bottom = shift(down3, 0, 1)
    from_left_head = shift(add(part["right_head"], to_right), 1, 0)
    from_right_tail = shift(add(part["left_tail"], to_left), -1, 0)
    top = shift(add(part["up2"], top), 0, -1)
    bottom = shift(add(part["down2"], bottom), 0, 1)
    col_head = add(part["col"][: 4 * SUB], from_left_head, from_right_head)
    col_tail = add(part["col"][4 * SUB :], from_left_tail, from_right_tail)
    below = shift(col_tail[2 * SUB : 3 * SUB], 0, -1)
    above = shift(col_tail[3 * SUB :], 0, 1)
    top = shift(add(part["up1"], top), 0, -1)
    bottom = shift(add(part["down1"], bottom), 0, 1)
    pair_down = jnp.concatenate(
        [add(col_head[2 * SUB : 3 * SUB], below), col_head[3 * SUB :]], axis=0
    )
    pair_up = jnp.concatenate([add(col_tail[:SUB], above), col_tail[SUB : 2 * SUB]], axis=0)
    pair = add(col_head[: 2 * SUB], shift(pair_down, 0, -1), shift(pair_up, 0, 1))
    row = add(part["row"], top, bottom)
    first = pair[:SUB].astype(jnp.float32) + shift(pair[SUB:], 0, 4).astype(jnp.float32)
    second = (
        row[:SUB].astype(jnp.float32)
        + shift(row[SUB : 2 * SUB], -1, 0).astype(jnp.float32)
        + shift(row[2 * SUB : 3 * SUB], 1, 0).astype(jnp.float32)
        + shift(row[3 * SUB :], 2, 0).astype(jnp.float32)
    )
    return jnp.concatenate([first, second], axis=0)


def project_kernel(sizes, offsets, *refs):
    count = len(sizes)
    chunk_refs = refs[:count]
    weight_out, residual, gain, weight_next = refs[count : count + 4]
    rows_in, rows_out, in_sems, out_sems = refs[-4:]
    hidden = refs[-5 - count]
    part_refs = refs[-4 - count : -4]
    starts = [sum(sizes[:i]) for i in range(count)]

    def fetch(sub):
        offset = pl.multiple_of(offsets[sub], SUB)
        return pltpu.make_async_copy(
            residual.at[pl.ds(offset, SUB)], rows_in.at[pl.ds(sub * SUB, SUB)], in_sems.at[sub]
        )

    def store(sub):
        offset = pl.multiple_of(offsets[sub], SUB)
        return pltpu.make_async_copy(
            rows_out.at[pl.ds(sub * SUB, SUB)], hidden.at[pl.ds(offset, SUB)], out_sems.at[sub]
        )

    subs = sum(sizes) // SUB
    for sub in range(subs):
        fetch(sub).start()
    for chunk, size, start, part in zip(chunk_refs, sizes, starts, part_refs):
        product = jnp.dot(chunk[...], weight_out[...], preferred_element_type=jnp.float32)
        for sub in range(start // SUB, (start + size) // SUB):
            fetch(sub).wait()
        rows = (rows_in[pl.ds(start, size)].astype(jnp.float32) + product).astype(jnp.bfloat16)
        rows_out[pl.ds(start, size)] = rows
        for sub in range(start // SUB, (start + size) // SUB):
            store(sub).start()
        wide = rows.astype(jnp.float32)
        scaled = (wide * gain[...].astype(jnp.float32)).astype(jnp.bfloat16)
        part[:, :QW] = jnp.dot(
            scaled, weight_next[...], preferred_element_type=jnp.float32
        ).astype(jnp.bfloat16)
        squares = jnp.sum(wide * wide, axis=1, keepdims=True)
        part[:, QW:] = jnp.broadcast_to(squares, (size, PW - QW)).astype(jnp.bfloat16)
    for sub in range(subs):
        store(sub).wait()


def project(chunks, offsets, weight_out, residual, gain, weight_next, hidden):
    sizes = [chunk.shape[0] for chunk in chunks]
    total = sum(sizes)
    width = weight_out.shape[1]
    vmem = pl.BlockSpec(memory_space=pltpu.VMEM)
    anywhere = pl.BlockSpec(memory_space=pl.ANY)
    outs = pl.pallas_call(
        functools.partial(project_kernel, sizes),
        out_shape=[jax.ShapeDtypeStruct(residual.shape, residual.dtype)]
        + [jax.ShapeDtypeStruct((size, PW), jnp.bfloat16) for size in sizes],
        in_specs=[pl.BlockSpec(memory_space=pltpu.SMEM)]
        + [vmem] * len(sizes)
        + [vmem, anywhere, vmem, vmem]
        + [anywhere] * len(hidden),
        out_specs=[anywhere] + [vmem] * len(sizes),
        scratch_shapes=[
            pltpu.VMEM((total, width), jnp.bfloat16),
            pltpu.VMEM((total, width), jnp.bfloat16),
            pltpu.SemaphoreType.DMA((total // SUB,)),
            pltpu.SemaphoreType.DMA((total // SUB,)),
        ],
        input_output_aliases={1 + len(sizes) + 4: 0} if hidden else {},
        compiler_params=pltpu.CompilerParams(vmem_limit_bytes=16 * 1024 * 1024),
        cost_estimate=pl.CostEstimate(
            flops=2 * total * width * (HQ * HD + QW),
            bytes_accessed=2 * total * (HQ * HD + 2 * width + PW) + 2 * width * (HQ * HD + QW),
            transcendentals=0,
        ),
    )(offsets, *chunks, weight_out, residual, gain, weight_next, *hidden)
    return outs[:1], outs[1:]


GROUPS = (
    ("row", "up1", "down1"),
    ("col", "left_head", "right_tail", "up2", "down2"),
    ("left_tail", "right_head", "up3", "down3"),
    ("far_head", "far_tail", "up4", "down4"),
)


def body(projected, positions, out_weight, residual, norm_gain, next_weight):
    local_rows = projected[0]
    tokens_here = local_rows.shape[0]
    outer = lax.axis_index("outer")
    inner = lax.axis_index("inner")
    here_x = outer % NX
    here_z = inner * 2 + outer // NX

    def offsets_of(runs):
        halves, dx, dz = (np.array(column, np.int32) for column in zip(*runs))
        return (shard_of(here_x + dx, here_z + dz) * 2 + halves) * SUB

    weight_next = section_shift(next_weight, -1)[0]
    gain = section_shift(norm_gain, -1)

    run_starts = positions[::SUB]
    query_starts = lax.dynamic_slice_in_dim(
        run_starts, shard_of(here_x, here_z) * 2, tokens_here // SUB
    )
    state = []
    groups = gather_rows(local_rows[:, HQ * HD :])
    for group in groups:
        runs = [
            (half, dx, dz) for _, order, dz in group for dx in order for half in range(2)
        ]
        state = attend(
            local_rows[:, : HQ * HD],
            [chunk for chunk, _, _ in group],
            jnp.take(run_starts, offsets_of(runs) // SUB),
            query_starts,
            state,
            group is groups[-1],
        )
    attended = state[0]

    chunks = gather(attended)
    hidden = []
    part = {}
    for names in GROUPS:
        offsets = offsets_of([run for name in names for run in chunks[name][1]])
        hidden, parts = project(
            [chunks[name][0] for name in names],
            offsets,
            out_weight[0],
            residual[0],
            gain,
            weight_next,
            hidden,
        )
        part.update(zip(names, parts))
    stream = section_shift(hidden[0][None], 1)
    summed = reduce_scatter(part)
    inverse_rms = lax.rsqrt(summed[:, QW : QW + 1] / D + 1e-05)
    result = (summed[:, :QW] * inverse_rms).astype(jnp.bfloat16)
    return (section_shift(result[None], 1), stream)


def solution(mesh):
    return jax.shard_map(
        body,
        mesh=mesh,
        in_specs=(
            P("section", ("outer", "inner"), None),
            P(),
            P("section", None, ("outer", "inner")),
            P("section", None, ("outer", "inner")),
            P("section", ("outer", "inner")),
            P("section", ("outer", "inner"), None),
        ),
        out_specs=(P("section", ("outer", "inner"), None), P("section", None, ("outer", "inner"))),
        check_vma=False,
    )
```

```python
import functools

import jax
import jax.numpy as jnp
import numpy as np
from jax import lax
from jax.experimental import pallas as pl
from jax.experimental.pallas import tpu as pltpu
from jax.sharding import PartitionSpec as P

D = 16384
HQ = 8
HD = 128
QW = 1280
SUB = 64
PW = QW + 128
NX = 4
NZ = 8
SHARD_AXES = ("outer", "inner")
Z_ORDER = (0, 4, -1, 3, 1, -3, -2, 2)
X_ORDER = (0, -1, 1, 2)
KEY_BLOCK = 256


def shard_of(x, z):
    x = x & (NX - 1)
    z = z & (NZ - 1)
    return (z & 1) * 16 + x * 4 + (z >> 1)


def shift(value, dx, dz):
    pairs = [
        (shard_of(x, z), shard_of(x + dx, z + dz)) for x in range(NX) for z in range(NZ)
    ]
    return lax.ppermute(value, SHARD_AXES, pairs)


def section_shift(value, by):
    return lax.ppermute(value, "section", [(i, (i + by) % 8) for i in range(8)])


def gather_rows(value):
    half = 2 * value.shape[0]
    left, right, far = shift(value, 1, 0), shift(value, -1, 0), shift(value, 2, 0)
    row = jnp.concatenate([value, left, right, far], axis=0)
    up1, down1 = shift(row, 0, 1), shift(row, 0, -1)
    up2, down2 = shift(up1, 0, 1), shift(down1, 0, -1)
    up3, down3 = shift(up2, 0, 1), shift(down2, 0, -1)
    up4, down4 = shift(up3[:half], 0, 1), shift(down3[half:], 0, -1)
    return (
        [(row, X_ORDER, 0)],
        [(up1, X_ORDER, -1), (down1, X_ORDER, 1)],
        [(up2, X_ORDER, -2), (down2, X_ORDER, 2)],
        [(up3, X_ORDER, -3), (down3, X_ORDER, 3)],
        [(up4, X_ORDER[:2], 4), (down4, X_ORDER[2:], 4)],
    )


def attend_kernel(sizes, is_first, is_last, key_starts, query_starts, *refs):
    count = len(sizes)
    queries = refs[0]
    chunks = refs[1 : count + 1]
    refs = refs[count + 1 :]
    tokens = queries.shape[0]
    columns = HQ * tokens
    if is_first:
        largest = jnp.full((1, columns), -1e30, jnp.float32)
        total = jnp.zeros((1, columns), jnp.float32)
        acc = jnp.zeros((HD, columns), jnp.float32)
    else:
        largest, total, acc = refs[0][...], refs[1][...], refs[2][...]
        refs = refs[3:]
    stacked = jnp.concatenate([queries[:, h * HD : (h + 1) * HD] for h in range(HQ)], axis=0)
    lane = lax.broadcasted_iota(jnp.int32, (1, tokens), 1)
    query_positions = lane
    for run in range(tokens // SUB):
        start = query_starts[run] - run * SUB
        query_positions = jnp.where(lane // SUB == run, lane + start, query_positions)
    row_index = lax.broadcasted_iota(jnp.int32, (SUB, tokens), 0)
    factor = HD ** (-0.5) * 1.4426950408889634
    run = 0
    for chunk, size in zip(chunks, sizes):
        for start in range(0, size, KEY_BLOCK):
            keys = chunk[pl.ds(start, KEY_BLOCK), :HD]
            values = chunk[pl.ds(start, KEY_BLOCK), HD:]
            scores = lax.dot_general(
                keys, stacked, (((1,), (1,)), ((), ())), preferred_element_type=jnp.float32
            )
            masked = []
            for part in range(KEY_BLOCK // SUB):
                visible = row_index + key_starts[run] <= query_positions
                visible = jnp.concatenate([visible] * HQ, axis=1)
                block = scores[part * SUB : (part + 1) * SUB] * factor
                masked.append(jnp.where(visible, block, -jnp.inf))
                run += 1
            masked = jnp.concatenate(masked, axis=0)
            new_largest = jnp.maximum(largest, jnp.max(masked, axis=0, keepdims=True))
            weights = jnp.exp2(masked - new_largest)
            keep = jnp.exp2(largest - new_largest)
            total = total * keep + jnp.sum(weights, axis=0, keepdims=True)
            acc = acc * keep + lax.dot_general(
                values,
                weights.astype(jnp.bfloat16),
                (((0,), (0,)), ((), ())),
                preferred_element_type=jnp.float32,
            )
            largest = new_largest
    if is_last:
        mixed = acc / total
        for h in range(HQ):
            refs[0][:, h * HD : (h + 1) * HD] = jnp.transpose(
                mixed[:, h * tokens : (h + 1) * tokens]
            ).astype(jnp.bfloat16)
    else:
        refs[0][...], refs[1][...], refs[2][...] = largest, total, acc


def attend(queries, chunks, key_starts, query_starts, state, is_last):
    sizes = [chunk.shape[0] for chunk in chunks]
    tokens = queries.shape[0]
    columns = HQ * tokens
    smem = pl.BlockSpec(memory_space=pltpu.SMEM)
    vmem = pl.BlockSpec(memory_space=pltpu.VMEM)
    if is_last:
        out_shape = [jax.ShapeDtypeStruct(queries.shape, jnp.bfloat16)]
    else:
        out_shape = [
            jax.ShapeDtypeStruct((1, columns), jnp.float32),
            jax.ShapeDtypeStruct((1, columns), jnp.float32),
            jax.ShapeDtypeStruct((HD, columns), jnp.float32),
        ]
    return pl.pallas_call(
        functools.partial(attend_kernel, sizes, not state, is_last),
        out_shape=out_shape,
        in_specs=[smem, smem] + [vmem] * (1 + len(chunks) + len(state)),
        out_specs=[vmem] * len(out_shape),
        compiler_params=pltpu.CompilerParams(vmem_limit_bytes=16 * 1024 * 1024),
        cost_estimate=pl.CostEstimate(
            flops=8 * sum(sizes) * columns * HD,
            bytes_accessed=4 * columns * HD,
            transcendentals=sum(sizes) * columns,
        ),
    )(key_starts, query_starts, queries, *chunks, *state)


def add(*terms):
    total = terms[0].astype(jnp.float32)
    for term in terms[1:]:
        total = total + term.astype(jnp.float32)
    return total.astype(jnp.bfloat16)


def project_kernel(sizes, offsets, *refs):
    count = len(sizes)
    chunk_refs = refs[:count]
    weight_out, residual, weight_next = refs[count : count + 3]
    rows_in, rows_out, in_sems, out_sems = refs[-4:]
    hidden = refs[-5 - count]
    part_refs = refs[-4 - count : -4]
    starts = [sum(sizes[:i]) for i in range(count)]

    def fetch(sub):
        offset = pl.multiple_of(offsets[sub], SUB)
        return pltpu.make_async_copy(
            residual.at[pl.ds(offset, SUB)], rows_in.at[pl.ds(sub * SUB, SUB)], in_sems.at[sub]
        )

    def store(sub):
        offset = pl.multiple_of(offsets[sub], SUB)
        return pltpu.make_async_copy(
            rows_out.at[pl.ds(sub * SUB, SUB)], hidden.at[pl.ds(offset, SUB)], out_sems.at[sub]
        )

    subs = sum(sizes) // SUB
    for sub in range(subs):
        fetch(sub).start()
    for chunk, size, start, part in zip(chunk_refs, sizes, starts, part_refs):
        product = jnp.dot(chunk[...], weight_out[...], preferred_element_type=jnp.float32)
        for sub in range(start // SUB, (start + size) // SUB):
            fetch(sub).wait()
        rows = (rows_in[pl.ds(start, size)].astype(jnp.float32) + product).astype(jnp.bfloat16)
        rows_out[pl.ds(start, size)] = rows
        for sub in range(start // SUB, (start + size) // SUB):
            store(sub).start()
        wide = rows.astype(jnp.float32)
        part[:, :QW] = jnp.dot(
            rows, weight_next[...], preferred_element_type=jnp.float32
        ).astype(jnp.bfloat16)
        squares = jnp.sum(wide * wide, axis=1, keepdims=True)
        part[:, QW:] = jnp.broadcast_to(squares, (size, PW - QW)).astype(jnp.bfloat16)
    for sub in range(subs):
        store(sub).wait()


def project(chunks, offsets, weight_out, residual, weight_next, hidden):
    sizes = [chunk.shape[0] for chunk in chunks]
    total = sum(sizes)
    width = weight_out.shape[1]
    vmem = pl.BlockSpec(memory_space=pltpu.VMEM)
    anywhere = pl.BlockSpec(memory_space=pl.ANY)
    outs = pl.pallas_call(
        functools.partial(project_kernel, sizes),
        out_shape=[jax.ShapeDtypeStruct(residual.shape, residual.dtype)]
        + [jax.ShapeDtypeStruct((size, PW), jnp.bfloat16) for size in sizes],
        in_specs=[pl.BlockSpec(memory_space=pltpu.SMEM)]
        + [vmem] * len(sizes)
        + [vmem, anywhere, vmem]
        + [anywhere] * len(hidden),
        out_specs=[anywhere] + [vmem] * len(sizes),
        scratch_shapes=[
            pltpu.VMEM((total, width), jnp.bfloat16),
            pltpu.VMEM((total, width), jnp.bfloat16),
            pltpu.SemaphoreType.DMA((total // SUB,)),
            pltpu.SemaphoreType.DMA((total // SUB,)),
        ],
        input_output_aliases={1 + len(sizes) + 3: 0} if hidden else {},
        compiler_params=pltpu.CompilerParams(vmem_limit_bytes=16 * 1024 * 1024),
        cost_estimate=pl.CostEstimate(
            flops=2 * total * width * (HQ * HD + QW),
            bytes_accessed=2 * total * (HQ * HD + 2 * width + PW) + 2 * width * (HQ * HD + QW),
            transcendentals=0,
        ),
    )(offsets, *chunks, weight_out, residual, weight_next, *hidden)
    return outs[:1], outs[1:]


def store_kernel(source, target, sem):
    copy = pltpu.make_async_copy(source, target, sem)
    copy.start()
    copy.wait()


def store(value):
    return pl.pallas_call(
        store_kernel,
        out_shape=jax.ShapeDtypeStruct(value.shape, value.dtype),
        in_specs=[pl.BlockSpec(memory_space=pl.ANY)],
        out_specs=pl.BlockSpec(memory_space=pltpu.HBM),
        scratch_shapes=[pltpu.SemaphoreType.DMA],
        cost_estimate=pl.CostEstimate(
            flops=0, bytes_accessed=4 * value.size, transcendentals=0
        ),
    )(value)


class Order:
    def __init__(self):
        self.last = None

    def tie(self, *values):
        if self.last is not None:
            *values, self.last = lax.optimization_barrier((*values, self.last))
        return values if len(values) > 1 else values[0]

    def done(self, *values):
        if self.last is not None:
            *values, _ = lax.optimization_barrier((*values, self.last))
        self.last = values[-1]
        return values if len(values) > 1 else values[0]


def exchange(attended, project_chunks, send_hidden):
    half_z = NZ // 2 * SUB
    first = attended[:SUB]
    second = attended[SUB:]

    def column(dx, order):
        return [(0, dx, dz) for dz in order]

    def line(order, dz):
        return [(1, dx, dz) for dx in order]

    opposite = shift(first, 0, 4)
    left, right, far = shift(second, 1, 0), shift(second, -1, 0), shift(second, 2, 0)
    pair = jnp.concatenate([first, opposite], axis=0)
    up, down = shift(pair, 0, 1), shift(pair, 0, -1)
    row = jnp.concatenate([second, left, right, far], axis=0)
    up1, down1 = shift(row, 0, 1), shift(row, 0, -1)
    (p_row,), (up, down) = project_chunks([row], line(X_ORDER, 0), [up, down])
    up_far, down_far = shift(up[:SUB], 0, 1), shift(down[:SUB], 0, -1)
    up2, down2 = shift(up1, 0, 1), shift(down1, 0, -1)
    col = jnp.concatenate([pair, up, down, up_far, down_far], axis=0)
    left, right = shift(col, 1, 0), shift(col, -1, 0)
    (p_up1, p_down1), (up2, down2) = project_chunks(
        [up1, down1], line(X_ORDER, -1) + line(X_ORDER, 1), [up2, down2]
    )
    up3, down3 = shift(up2, 0, 1), shift(down2, 0, -1)
    (p_col, p_up2, p_down2), (left, right, up3, down3) = project_chunks(
        [col, up2, down2],
        column(0, Z_ORDER) + line(X_ORDER, -2) + line(X_ORDER, 2),
        [left, right, up3, down3],
    )
    up4, down4 = shift(up3[: 2 * SUB], 0, 1), shift(down3[2 * SUB :], 0, -1)
    far_head, far_tail = shift(left[:half_z], 1, 0), shift(right[half_z:], -1, 0)
    (p_left, p_right, p_up3, p_down3), (far_head, far_tail, up4, down4) = project_chunks(
        [left, right, up3, down3],
        column(-1, Z_ORDER) + column(1, Z_ORDER) + line(X_ORDER, -3) + line(X_ORDER, 3),
        [far_head, far_tail, up4, down4],
    )
    (p_far_head, p_far_tail), (up4, down4) = project_chunks(
        [far_head, far_tail],
        column(2, Z_ORDER[: NZ // 2]) + column(2, Z_ORDER[NZ // 2 :]),
        [up4, down4],
    )
    from_left = shift(jnp.concatenate([p_far_head, p_right[half_z:]], axis=0), 1, 0)
    from_right = shift(jnp.concatenate([p_far_tail, p_left[:half_z]], axis=0), -1, 0)
    (p_up4, p_down4), _ = project_chunks(
        [up4, down4], line(X_ORDER[:2], 4) + line(X_ORDER[2:], 4), []
    )
    top, bottom = shift(p_up4, 0, -1), shift(p_down4, 0, 1)

    order = Order()
    p_up3 = jnp.concatenate([add(p_up3[: 2 * SUB], top), p_up3[2 * SUB :]], axis=0)
    p_down3 = jnp.concatenate([p_down3[: 2 * SUB], add(p_down3[2 * SUB :], bottom)], axis=0)
    p_up3, p_down3 = order.done(p_up3, p_down3)
    top, bottom = shift(p_up3, 0, -1), shift(p_down3, 0, 1)
    stream = send_hidden(order)
    p_up2, p_down2 = order.tie(p_up2, p_down2)
    p_up2, p_down2 = order.done(add(p_up2, top), add(p_down2, bottom))
    top, bottom = shift(p_up2, 0, -1), shift(p_down2, 0, 1)
    p_left, p_right = order.tie(p_left, p_right)
    p_right, p_left = order.done(
        add(p_right[:half_z], from_left[:half_z]), add(p_left[half_z:], from_right[:half_z])
    )
    from_left_head, from_right_tail = shift(p_right, 1, 0), shift(p_left, -1, 0)
    p_up1, p_down1 = order.tie(p_up1, p_down1)
    p_up1, p_down1 = order.done(add(p_up1, top), add(p_down1, bottom))
    top, bottom = shift(p_up1, 0, -1), shift(p_down1, 0, 1)
    p_col = order.tie(p_col)
    p_head, p_tail = order.done(
        add(p_col[:half_z], from_left_head, from_right[half_z:]),
        add(p_col[half_z:], from_left[half_z:], from_right_tail),
    )
    below = shift(p_tail[2 * SUB : 3 * SUB], 0, -1)
    above = shift(p_tail[3 * SUB :], 0, 1)
    p_row, stream = order.tie(p_row, stream)
    row = order.done(add(p_row, top, bottom))
    terms = [
        row[:SUB],
        shift(row[SUB : 2 * SUB], -1, 0),
        shift(row[2 * SUB : 3 * SUB], 1, 0),
        shift(row[3 * SUB :], 2, 0),
    ]
    p_head, p_tail = order.tie(p_head, p_tail)
    pair_down = jnp.concatenate(
        [add(p_head[2 * SUB : 3 * SUB], below), p_head[3 * SUB :]], axis=0
    )
    pair_up = jnp.concatenate([add(p_tail[:SUB], above), p_tail[SUB : 2 * SUB]], axis=0)
    pair_down, pair_up = order.done(pair_down, pair_up)
    from_above, from_below = shift(pair_down, 0, -1), shift(pair_up, 0, 1)
    pair = add(p_head[: 2 * SUB], from_above, from_below)
    first = pair[:SUB].astype(jnp.float32) + shift(pair[SUB:], 0, 4).astype(jnp.float32)
    second = sum(term.astype(jnp.float32) for term in terms)
    return jnp.concatenate([first, second], axis=0), stream


def body(projected, positions, out_weight, residual, norm_gain, next_weight):
    local_rows = projected[0]
    tokens_here = local_rows.shape[0]
    outer = lax.axis_index("outer")
    inner = lax.axis_index("inner")
    here_x = outer % NX
    here_z = inner * 2 + outer // NX

    def offsets_of(runs):
        halves, dx, dz = (np.array(column, np.int32) for column in zip(*runs))
        return (shard_of(here_x + dx, here_z + dz) * 2 + halves) * SUB

    scaled = next_weight[0].astype(jnp.float32) * norm_gain[0].astype(jnp.float32)[:, None]
    weight_next = section_shift(scaled.astype(jnp.bfloat16), -1)

    run_starts = positions[::SUB]
    query_starts = lax.dynamic_slice_in_dim(
        run_starts, shard_of(here_x, here_z) * 2, tokens_here // SUB
    )
    state = []
    groups = gather_rows(local_rows[:, HQ * HD :])
    for group in groups:
        runs = [
            (half, dx, dz) for _, order, dz in group for dx in order for half in range(2)
        ]
        state = attend(
            local_rows[:, : HQ * HD],
            [chunk for chunk, _, _ in group],
            jnp.take(run_starts, offsets_of(runs) // SUB),
            query_starts,
            state,
            group is groups[-1],
        )
    attended = state[0]

    hidden = []

    def project_chunks(chunks, runs, held):
        outs, parts = project(
            chunks, offsets_of(runs), out_weight[0], residual[0], weight_next, hidden
        )
        outs = list(outs)
        if held:
            outs[0], held = lax.optimization_barrier((outs[0], held))
        hidden[:] = outs
        return parts, held

    def send_hidden(order):
        return section_shift(order.tie(hidden[0])[None], 1)

    summed, stream = exchange(attended, project_chunks, send_hidden)
    inverse_rms = lax.rsqrt(summed[:, QW : QW + 1] / D + 1e-05)
    result = (summed[:, :QW] * inverse_rms).astype(jnp.bfloat16)
    return (section_shift(result[None], 1), store(stream))


def solution(mesh):
    return jax.shard_map(
        body,
        mesh=mesh,
        in_specs=(
            P("section", ("outer", "inner"), None),
            P(),
            P("section", None, ("outer", "inner")),
            P("section", None, ("outer", "inner")),
            P("section", ("outer", "inner")),
            P("section", ("outer", "inner"), None),
        ),
        out_specs=(P("section", ("outer", "inner"), None), P("section", None, ("outer", "inner"))),
        check_vma=False,
    )
```

```python
import functools

import jax
import jax.numpy as jnp
import numpy as np
from jax import lax
from jax.experimental import pallas as pl
from jax.experimental.pallas import tpu as pltpu
from jax.sharding import PartitionSpec as P

D = 16384
HQ = 8
HD = 128
QW = 1280
SUB = 64
PW = QW + 128
NX = 4
NZ = 8
SHARD_AXES = ("outer", "inner")
Z_ORDER = (0, 4, -1, 3, 1, -3, -2, 2)
X_ORDER = (0, -1, 1, 2)
KEY_BLOCK = 256


def shard_of(x, z):
    x = x & (NX - 1)
    z = z & (NZ - 1)
    return (z & 1) * 16 + x * 4 + (z >> 1)


def shift(value, dx, dz):
    pairs = [
        (shard_of(x, z), shard_of(x + dx, z + dz)) for x in range(NX) for z in range(NZ)
    ]
    return lax.ppermute(value, SHARD_AXES, pairs)


def section_shift(value, by):
    return lax.ppermute(value, "section", [(i, (i + by) % 8) for i in range(8)])


def gather_rows(value):
    half = 2 * value.shape[0]
    left, right, far = shift(value, 1, 0), shift(value, -1, 0), shift(value, 2, 0)
    row = jnp.concatenate([value, left, right, far], axis=0)
    up1, down1 = shift(row, 0, 1), shift(row, 0, -1)
    up2, down2 = shift(up1, 0, 1), shift(down1, 0, -1)
    up3, down3 = shift(up2, 0, 1), shift(down2, 0, -1)
    up4, down4 = shift(up3[:half], 0, 1), shift(down3[half:], 0, -1)
    return (
        [(row, X_ORDER, 0)],
        [(up1, X_ORDER, -1), (down1, X_ORDER, 1)],
        [(up2, X_ORDER, -2), (down2, X_ORDER, 2)],
        [(up3, X_ORDER, -3), (down3, X_ORDER, 3)],
        [(up4, X_ORDER[:2], 4), (down4, X_ORDER[2:], 4)],
    )


def attend_kernel(sizes, is_first, is_last, key_starts, query_starts, *refs):
    count = len(sizes)
    queries = refs[0]
    chunks = refs[1 : count + 1]
    refs = refs[count + 1 :]
    tokens = queries.shape[0]
    columns = HQ * tokens
    if is_first:
        largest = jnp.full((1, columns), -1e30, jnp.float32)
        total = jnp.zeros((1, columns), jnp.float32)
        acc = jnp.zeros((HD, columns), jnp.float32)
    else:
        largest, total, acc = refs[0][...], refs[1][...], refs[2][...]
        refs = refs[3:]
    stacked = jnp.concatenate([queries[:, h * HD : (h + 1) * HD] for h in range(HQ)], axis=0)
    lane = lax.broadcasted_iota(jnp.int32, (1, tokens), 1)
    query_positions = lane
    for run in range(tokens // SUB):
        start = query_starts[run] - run * SUB
        query_positions = jnp.where(lane // SUB == run, lane + start, query_positions)
    row_index = lax.broadcasted_iota(jnp.int32, (SUB, tokens), 0)
    factor = HD ** (-0.5) * 1.4426950408889634
    run = 0
    for chunk, size in zip(chunks, sizes):
        for start in range(0, size, KEY_BLOCK):
            keys = chunk[pl.ds(start, KEY_BLOCK), :HD]
            values = chunk[pl.ds(start, KEY_BLOCK), HD:]
            scores = lax.dot_general(
                keys, stacked, (((1,), (1,)), ((), ())), preferred_element_type=jnp.float32
            )
            masked = []
            for part in range(KEY_BLOCK // SUB):
                visible = row_index + key_starts[run] <= query_positions
                visible = jnp.concatenate([visible] * HQ, axis=1)
                block = scores[part * SUB : (part + 1) * SUB] * factor
                masked.append(jnp.where(visible, block, -jnp.inf))
                run += 1
            masked = jnp.concatenate(masked, axis=0)
            new_largest = jnp.maximum(largest, jnp.max(masked, axis=0, keepdims=True))
            weights = jnp.exp2(masked - new_largest)
            keep = jnp.exp2(largest - new_largest)
            total = total * keep + jnp.sum(weights, axis=0, keepdims=True)
            acc = acc * keep + lax.dot_general(
                values,
                weights.astype(jnp.bfloat16),
                (((0,), (0,)), ((), ())),
                preferred_element_type=jnp.float32,
            )
            largest = new_largest
    if is_last:
        mixed = acc / total
        for h in range(HQ):
            refs[0][:, h * HD : (h + 1) * HD] = jnp.transpose(
                mixed[:, h * tokens : (h + 1) * tokens]
            ).astype(jnp.bfloat16)
    else:
        refs[0][...], refs[1][...], refs[2][...] = largest, total, acc


def attend(queries, chunks, key_starts, query_starts, state, is_last):
    sizes = [chunk.shape[0] for chunk in chunks]
    tokens = queries.shape[0]
    columns = HQ * tokens
    smem = pl.BlockSpec(memory_space=pltpu.SMEM)
    vmem = pl.BlockSpec(memory_space=pltpu.VMEM)
    if is_last:
        out_shape = [jax.ShapeDtypeStruct(queries.shape, jnp.bfloat16)]
    else:
        out_shape = [
            jax.ShapeDtypeStruct((1, columns), jnp.float32),
            jax.ShapeDtypeStruct((1, columns), jnp.float32),
            jax.ShapeDtypeStruct((HD, columns), jnp.float32),
        ]
    return pl.pallas_call(
        functools.partial(attend_kernel, sizes, not state, is_last),
        out_shape=out_shape,
        in_specs=[smem, smem] + [vmem] * (1 + len(chunks) + len(state)),
        out_specs=[vmem] * len(out_shape),
        compiler_params=pltpu.CompilerParams(vmem_limit_bytes=16 * 1024 * 1024),
        cost_estimate=pl.CostEstimate(
            flops=8 * sum(sizes) * columns * HD,
            bytes_accessed=4 * columns * HD,
            transcendentals=sum(sizes) * columns,
        ),
    )(key_starts, query_starts, queries, *chunks, *state)


def add(*terms):
    total = terms[0].astype(jnp.float32)
    for term in terms[1:]:
        total = total + term.astype(jnp.float32)
    return total.astype(jnp.bfloat16)


def project_kernel(sizes, offsets, *refs):
    count = len(sizes)
    chunk_refs = refs[:count]
    weight_out, residual, weight_next = refs[count : count + 3]
    rows_in, rows_out, in_sems, out_sems = refs[-4:]
    hidden = refs[-5 - count]
    part_refs = refs[-4 - count : -4]
    starts = [sum(sizes[:i]) for i in range(count)]

    def fetch(sub):
        offset = pl.multiple_of(offsets[sub], SUB)
        return pltpu.make_async_copy(
            residual.at[pl.ds(offset, SUB)], rows_in.at[pl.ds(sub * SUB, SUB)], in_sems.at[sub]
        )

    def store(sub):
        offset = pl.multiple_of(offsets[sub], SUB)
        return pltpu.make_async_copy(
            rows_out.at[pl.ds(sub * SUB, SUB)], hidden.at[pl.ds(offset, SUB)], out_sems.at[sub]
        )

    subs = sum(sizes) // SUB
    for sub in range(subs):
        fetch(sub).start()
    for chunk, size, start, part in zip(chunk_refs, sizes, starts, part_refs):
        product = jnp.dot(chunk[...], weight_out[...], preferred_element_type=jnp.float32)
        for sub in range(start // SUB, (start + size) // SUB):
            fetch(sub).wait()
        rows = (rows_in[pl.ds(start, size)].astype(jnp.float32) + product).astype(jnp.bfloat16)
        rows_out[pl.ds(start, size)] = rows
        for sub in range(start // SUB, (start + size) // SUB):
            store(sub).start()
        wide = rows.astype(jnp.float32)
        part[:, :QW] = jnp.dot(
            rows, weight_next[...], preferred_element_type=jnp.float32
        ).astype(jnp.bfloat16)
        squares = jnp.sum(wide * wide, axis=1, keepdims=True)
        part[:, QW:] = jnp.broadcast_to(squares, (size, PW - QW)).astype(jnp.bfloat16)
    for sub in range(subs):
        store(sub).wait()


def project(chunks, offsets, weight_out, residual, weight_next, hidden):
    sizes = [chunk.shape[0] for chunk in chunks]
    total = sum(sizes)
    width = weight_out.shape[1]
    vmem = pl.BlockSpec(memory_space=pltpu.VMEM)
    anywhere = pl.BlockSpec(memory_space=pl.ANY)
    outs = pl.pallas_call(
        functools.partial(project_kernel, sizes),
        out_shape=[jax.ShapeDtypeStruct(residual.shape, residual.dtype)]
        + [jax.ShapeDtypeStruct((size, PW), jnp.bfloat16) for size in sizes],
        in_specs=[pl.BlockSpec(memory_space=pltpu.SMEM)]
        + [vmem] * len(sizes)
        + [vmem, anywhere, vmem]
        + [anywhere] * len(hidden),
        out_specs=[anywhere] + [vmem] * len(sizes),
        scratch_shapes=[
            pltpu.VMEM((total, width), jnp.bfloat16),
            pltpu.VMEM((total, width), jnp.bfloat16),
            pltpu.SemaphoreType.DMA((total // SUB,)),
            pltpu.SemaphoreType.DMA((total // SUB,)),
        ],
        input_output_aliases={1 + len(sizes) + 3: 0} if hidden else {},
        compiler_params=pltpu.CompilerParams(vmem_limit_bytes=16 * 1024 * 1024),
        cost_estimate=pl.CostEstimate(
            flops=2 * total * width * (HQ * HD + QW),
            bytes_accessed=2 * total * (HQ * HD + 2 * width + PW) + 2 * width * (HQ * HD + QW),
            transcendentals=0,
        ),
    )(offsets, *chunks, weight_out, residual, weight_next, *hidden)
    return outs[:1], outs[1:]


class Order:
    def __init__(self):
        self.last = None

    def tie(self, *values):
        if self.last is not None:
            *values, self.last = lax.optimization_barrier((*values, self.last))
        return values if len(values) > 1 else values[0]

    def done(self, *values):
        if self.last is not None:
            *values, _ = lax.optimization_barrier((*values, self.last))
        self.last = values[-1]
        return values if len(values) > 1 else values[0]


def exchange(attended, project_chunks, send_hidden):
    half_z = NZ // 2 * SUB
    first = attended[:SUB]
    second = attended[SUB:]

    def column(dx, order):
        return [(0, dx, dz) for dz in order]

    def line(order, dz):
        return [(1, dx, dz) for dx in order]

    opposite = shift(first, 0, 4)
    left, right, far = shift(second, 1, 0), shift(second, -1, 0), shift(second, 2, 0)
    pair = jnp.concatenate([first, opposite], axis=0)
    up, down = shift(pair, 0, 1), shift(pair, 0, -1)
    row = jnp.concatenate([second, left, right, far], axis=0)
    up1, down1 = shift(row, 0, 1), shift(row, 0, -1)
    (p_row,), (up, down) = project_chunks([row], line(X_ORDER, 0), [up, down])
    up_far, down_far = shift(up[:SUB], 0, 1), shift(down[:SUB], 0, -1)
    up2, down2 = shift(up1, 0, 1), shift(down1, 0, -1)
    col = jnp.concatenate([pair, up, down, up_far, down_far], axis=0)
    left, right = shift(col, 1, 0), shift(col, -1, 0)
    (p_up1, p_down1), (up2, down2) = project_chunks(
        [up1, down1], line(X_ORDER, -1) + line(X_ORDER, 1), [up2, down2]
    )
    up3, down3 = shift(up2, 0, 1), shift(down2, 0, -1)
    (p_col, p_up2, p_down2), (left, right, up3, down3) = project_chunks(
        [col, up2, down2],
        column(0, Z_ORDER) + line(X_ORDER, -2) + line(X_ORDER, 2),
        [left, right, up3, down3],
    )
    up4, down4 = shift(up3[: 2 * SUB], 0, 1), shift(down3[2 * SUB :], 0, -1)
    far_head, far_tail = shift(left[:half_z], 1, 0), shift(right[half_z:], -1, 0)
    (p_left, p_right, p_up3, p_down3), (far_head, far_tail, up4, down4) = project_chunks(
        [left, right, up3, down3],
        column(-1, Z_ORDER) + column(1, Z_ORDER) + line(X_ORDER, -3) + line(X_ORDER, 3),
        [far_head, far_tail, up4, down4],
    )
    (p_far_head, p_far_tail), (up4, down4) = project_chunks(
        [far_head, far_tail],
        column(2, Z_ORDER[: NZ // 2]) + column(2, Z_ORDER[NZ // 2 :]),
        [up4, down4],
    )
    from_left = shift(jnp.concatenate([p_far_head, p_right[half_z:]], axis=0), 1, 0)
    from_right = shift(jnp.concatenate([p_far_tail, p_left[:half_z]], axis=0), -1, 0)
    (p_up4, p_down4), _ = project_chunks(
        [up4, down4], line(X_ORDER[:2], 4) + line(X_ORDER[2:], 4), []
    )
    top, bottom = shift(p_up4, 0, -1), shift(p_down4, 0, 1)

    order = Order()
    p_up3 = jnp.concatenate([add(p_up3[: 2 * SUB], top), p_up3[2 * SUB :]], axis=0)
    p_down3 = jnp.concatenate([p_down3[: 2 * SUB], add(p_down3[2 * SUB :], bottom)], axis=0)
    p_up3, p_down3 = order.done(p_up3, p_down3)
    top, bottom = shift(p_up3, 0, -1), shift(p_down3, 0, 1)
    stream = send_hidden(order)
    p_up2, p_down2 = order.tie(p_up2, p_down2)
    p_up2, p_down2 = order.done(add(p_up2, top), add(p_down2, bottom))
    top, bottom = shift(p_up2, 0, -1), shift(p_down2, 0, 1)
    p_left, p_right = order.tie(p_left, p_right)
    p_right, p_left = order.done(
        add(p_right[:half_z], from_left[:half_z]), add(p_left[half_z:], from_right[:half_z])
    )
    from_left_head, from_right_tail = shift(p_right, 1, 0), shift(p_left, -1, 0)
    p_up1, p_down1 = order.tie(p_up1, p_down1)
    p_up1, p_down1 = order.done(add(p_up1, top), add(p_down1, bottom))
    top, bottom = shift(p_up1, 0, -1), shift(p_down1, 0, 1)
    p_col = order.tie(p_col)
    p_head, p_tail = order.done(
        add(p_col[:half_z], from_left_head, from_right[half_z:]),
        add(p_col[half_z:], from_left[half_z:], from_right_tail),
    )
    below = shift(p_tail[2 * SUB : 3 * SUB], 0, -1)
    above = shift(p_tail[3 * SUB :], 0, 1)
    p_row, stream = order.tie(p_row, stream)
    row = order.done(add(p_row, top, bottom))
    terms = [
        row[:SUB],
        shift(row[SUB : 2 * SUB], -1, 0),
        shift(row[2 * SUB : 3 * SUB], 1, 0),
        shift(row[3 * SUB :], 2, 0),
    ]
    p_head, p_tail = order.tie(p_head, p_tail)
    pair_down = jnp.concatenate(
        [add(p_head[2 * SUB : 3 * SUB], below), p_head[3 * SUB :]], axis=0
    )
    pair_up = jnp.concatenate([add(p_tail[:SUB], above), p_tail[SUB : 2 * SUB]], axis=0)
    pair_down, pair_up = order.done(pair_down, pair_up)
    from_above, from_below = shift(pair_down, 0, -1), shift(pair_up, 0, 1)
    pair = add(p_head[: 2 * SUB], from_above, from_below)
    first = pair[:SUB].astype(jnp.float32) + shift(pair[SUB:], 0, 4).astype(jnp.float32)
    second = sum(term.astype(jnp.float32) for term in terms)
    return jnp.concatenate([first, second], axis=0), stream


def body(projected, positions, out_weight, residual, norm_gain, next_weight):
    local_rows = projected[0]
    tokens_here = local_rows.shape[0]
    outer = lax.axis_index("outer")
    inner = lax.axis_index("inner")
    here_x = outer % NX
    here_z = inner * 2 + outer // NX

    def offsets_of(runs):
        halves, dx, dz = (np.array(column, np.int32) for column in zip(*runs))
        return (shard_of(here_x + dx, here_z + dz) * 2 + halves) * SUB

    scaled = next_weight[0].astype(jnp.float32) * norm_gain[0].astype(jnp.float32)[:, None]
    weight_next = section_shift(scaled.astype(jnp.bfloat16), -1)

    run_starts = positions[::SUB]
    query_starts = lax.dynamic_slice_in_dim(
        run_starts, shard_of(here_x, here_z) * 2, tokens_here // SUB
    )
    state = []
    groups = gather_rows(local_rows[:, HQ * HD :])
    for group in groups:
        runs = [
            (half, dx, dz) for _, order, dz in group for dx in order for half in range(2)
        ]
        state = attend(
            local_rows[:, : HQ * HD],
            [chunk for chunk, _, _ in group],
            jnp.take(run_starts, offsets_of(runs) // SUB),
            query_starts,
            state,
            group is groups[-1],
        )
    attended = state[0]

    hidden = []

    def project_chunks(chunks, runs, held):
        outs, parts = project(
            chunks, offsets_of(runs), out_weight[0], residual[0], weight_next, hidden
        )
        outs = list(outs)
        if held:
            outs[0], held = lax.optimization_barrier((outs[0], held))
        hidden[:] = outs
        return parts, held

    def send_hidden(order):
        return section_shift(order.tie(hidden[0])[None], 1)

    summed, stream = exchange(attended, project_chunks, send_hidden)
    inverse_rms = lax.rsqrt(summed[:, QW : QW + 1] / D + 1e-05)
    result = (summed[:, :QW] * inverse_rms).astype(jnp.bfloat16)
    return (section_shift(result[None], 1), stream)


def solution(mesh):
    return jax.shard_map(
        body,
        mesh=mesh,
        in_specs=(
            P("section", ("outer", "inner"), None),
            P(),
            P("section", None, ("outer", "inner")),
            P("section", None, ("outer", "inner")),
            P("section", ("outer", "inner")),
            P("section", ("outer", "inner"), None),
        ),
        out_specs=(P("section", ("outer", "inner"), None), P("section", None, ("outer", "inner"))),
        check_vma=False,
    )
```

```python
import functools

import jax
import jax.numpy as jnp
from jax import lax
from jax.experimental import pallas as pl
from jax.experimental.pallas import tpu as pltpu
from jax.sharding import PartitionSpec as P

D = 16384
HQ = 8
HD = 128
QW = 1280
SUB = 64
PW = QW + 128
NX = 4
NZ = 8
SHARD_AXES = ("outer", "inner")
Z_ORDER = (0, 4, -1, 3, 1, -3, -2, 2)
X_ORDER = (0, -1, 1, 2)
KEY_BLOCK = 256
VMEM_GRANT = 12 * 1024 * 1024


def shard_of(x, z):
    x = x & (NX - 1)
    z = z & (NZ - 1)
    return (z & 1) * 16 + x * 4 + (z >> 1)


def run_of(here, half, dx, dz):
    return shard_of(here[0] + dx, here[1] + dz) * 2 + half


def shift(value, dx, dz):
    pairs = [
        (shard_of(x, z), shard_of(x + dx, z + dz)) for x in range(NX) for z in range(NZ)
    ]
    return lax.ppermute(value, SHARD_AXES, pairs)


def section_shift(value, by):
    return lax.ppermute(value, "section", [(i, (i + by) % 8) for i in range(8)])


def attend_kernel(sizes, runs, is_first, is_last, here, run_starts, *refs):
    count = len(sizes)
    rows = refs[0]
    chunks = refs[1 : count + 1]
    refs = refs[count + 1 :]
    tokens = rows.shape[0]
    columns = HQ * tokens
    if is_first:
        largest = jnp.full((1, columns), -1e30, jnp.float32)
        total = jnp.zeros((1, columns), jnp.float32)
        acc = jnp.zeros((HD, columns), jnp.float32)
    else:
        largest, total, acc = refs[0][...], refs[1][...], refs[2][...]
        refs = refs[3:]
    stacked = jnp.concatenate([rows[:, h * HD : (h + 1) * HD] for h in range(HQ)], axis=0)
    lane = lax.broadcasted_iota(jnp.int32, (1, tokens), 1)
    query_positions = lane
    for run in range(tokens // SUB):
        start = run_starts[run_of(here, run, 0, 0)] - run * SUB
        query_positions = jnp.where(lane // SUB == run, lane + start, query_positions)
    row_index = lax.broadcasted_iota(jnp.int32, (SUB, tokens), 0)
    factor = HD ** (-0.5) * 1.4426950408889634
    run = 0
    for chunk, size in zip(chunks, sizes):
        for start in range(0, size, KEY_BLOCK):
            keys = chunk[pl.ds(start, KEY_BLOCK), :HD]
            values = chunk[pl.ds(start, KEY_BLOCK), HD:]
            scores = lax.dot_general(
                keys, stacked, (((1,), (1,)), ((), ())), preferred_element_type=jnp.float32
            )
            masked = []
            for part in range(KEY_BLOCK // SUB):
                start_here = run_starts[run_of(here, *runs[run])]
                visible = row_index + start_here <= query_positions
                visible = jnp.concatenate([visible] * HQ, axis=1)
                block = scores[part * SUB : (part + 1) * SUB] * factor
                masked.append(jnp.where(visible, block, -jnp.inf))
                run += 1
            masked = jnp.concatenate(masked, axis=0)
            new_largest = jnp.maximum(largest, jnp.max(masked, axis=0, keepdims=True))
            weights = jnp.exp2(masked - new_largest)
            keep = jnp.exp2(largest - new_largest)
            total = total * keep + jnp.sum(weights, axis=0, keepdims=True)
            acc = acc * keep + lax.dot_general(
                values,
                weights.astype(jnp.bfloat16),
                (((0,), (0,)), ((), ())),
                preferred_element_type=jnp.float32,
            )
            largest = new_largest
    if is_last:
        mixed = acc / total
        for h in range(HQ):
            turned = jnp.transpose(mixed[:, h * tokens : (h + 1) * tokens]).astype(jnp.bfloat16)
            for half in range(2):
                refs[half][:, h * HD : (h + 1) * HD] = turned[half * SUB : (half + 1) * SUB]
    else:
        refs[0][...], refs[1][...], refs[2][...] = largest, total, acc


def attend(here, run_starts, rows, chunks, runs, state, is_last=False):
    sizes = [chunk.shape[0] for chunk in chunks]
    columns = HQ * rows.shape[0]
    smem = pl.BlockSpec(memory_space=pltpu.SMEM)
    vmem = pl.BlockSpec(memory_space=pltpu.VMEM)
    if is_last:
        out_shape = [jax.ShapeDtypeStruct((SUB, HQ * HD), jnp.bfloat16)] * 2
    else:
        out_shape = [
            jax.ShapeDtypeStruct((1, columns), jnp.float32),
            jax.ShapeDtypeStruct((1, columns), jnp.float32),
            jax.ShapeDtypeStruct((HD, columns), jnp.float32),
        ]
    return pl.pallas_call(
        functools.partial(attend_kernel, sizes, runs, not state, is_last),
        out_shape=out_shape,
        in_specs=[smem, smem] + [vmem] * (1 + len(chunks) + len(state)),
        out_specs=[vmem] * len(out_shape),
        compiler_params=pltpu.CompilerParams(vmem_limit_bytes=16 * 1024 * 1024),
        cost_estimate=pl.CostEstimate(
            flops=8 * sum(sizes) * columns * HD,
            bytes_accessed=4 * columns * HD,
            transcendentals=sum(sizes) * columns,
        ),
    )(here, run_starts, rows, *chunks, *state)


def attention(here, run_starts, rows):
    key_value = rows[:, HQ * HD :]
    tokens = rows.shape[0]
    left, right, far = shift(key_value, 1, 0), shift(key_value, -1, 0), shift(key_value, 2, 0)
    row = jnp.concatenate([key_value, left, right, far], axis=0)
    step = functools.partial(attend, here, run_starts, rows)

    def line(dz, order=X_ORDER):
        return [(half, dx, dz) for dx in order for half in range(2)]

    up, down = shift(row, 0, 1), shift(row, 0, -1)
    state = step([row], line(0), [])
    for dz in (1, 2, 3):
        up, down, state = lax.optimization_barrier((up, down, state))
        if dz < 3:
            next_up, next_down = shift(up, 0, 1), shift(down, 0, -1)
        else:
            next_up = shift(up[: 2 * tokens], 0, 1)
            next_down = shift(down[2 * tokens :], 0, -1)
        state = step([up, down], line(-dz) + line(dz), state)
        up, down = next_up, next_down
    return step([up, down], line(4, X_ORDER[:2]) + line(4, X_ORDER[2:]), state, True)


def add(*terms):
    total = terms[0].astype(jnp.float32)
    for term in terms[1:]:
        total = total + term.astype(jnp.float32)
    return total.astype(jnp.bfloat16)


def project_kernel(pieces, kept, here, *refs):
    weight_out, residual, weight_next = refs[:3]
    chunks = refs[3 : 3 + len({piece[0] for piece in pieces})]
    outs = refs[3 + len(chunks) + kept :]
    hidden, parts = outs[0], outs[1:]
    for chunk, start, runs, part, part_start in pieces:
        size = len(runs) * SUB
        product = jnp.dot(
            chunks[chunk][pl.ds(start, size)], weight_out[...], preferred_element_type=jnp.float32
        )
        rows = []
        for sub, run in enumerate(runs):
            offset = pl.multiple_of(run_of(here, *run) * SUB, SUB)
            sums = residual[pl.ds(offset, SUB)].astype(jnp.float32)
            sums = (sums + product[sub * SUB : (sub + 1) * SUB]).astype(jnp.bfloat16)
            hidden[pl.ds(offset, SUB)] = sums
            rows.append(sums)
        rows = jnp.concatenate(rows, axis=0)
        place = pl.ds(part_start, size)
        parts[part][place, :QW] = jnp.dot(
            rows, weight_next[...], preferred_element_type=jnp.float32
        ).astype(jnp.bfloat16)
        wide = rows.astype(jnp.float32)
        squares = jnp.sum(wide * wide, axis=1, keepdims=True)
        parts[part][place, QW:] = jnp.broadcast_to(squares, (size, PW - QW)).astype(jnp.bfloat16)


def project(here, weights, residual, hidden, chunks, pieces, part_rows, started=()):
    total = sum(len(piece[2]) for piece in pieces) * SUB
    width = residual.shape[1]
    kept = [*hidden, *started]
    vmem = pl.BlockSpec(memory_space=pltpu.VMEM)
    hidden, *parts = pl.pallas_call(
        functools.partial(project_kernel, pieces, len(kept)),
        out_shape=[jax.ShapeDtypeStruct(residual.shape, residual.dtype)]
        + [jax.ShapeDtypeStruct((rows, PW), jnp.bfloat16) for rows in part_rows],
        in_specs=[pl.BlockSpec(memory_space=pltpu.SMEM)]
        + [vmem] * (3 + len(chunks) + len(kept)),
        out_specs=[vmem] * (1 + len(part_rows)),
        input_output_aliases={4 + len(chunks) + i: i for i in range(len(kept))},
        compiler_params=pltpu.CompilerParams(vmem_limit_bytes=VMEM_GRANT),
        cost_estimate=pl.CostEstimate(
            flops=2 * total * width * (HQ * HD + QW),
            bytes_accessed=2 * total * (HQ * HD + 2 * width + PW) + 2 * width * (HQ * HD + QW),
            transcendentals=0,
        ),
    )(here, weights[0], residual, weights[1], *chunks, *kept)
    return [hidden], parts


class Order:
    def __init__(self):
        self.last = None

    def tie(self, *values):
        if self.last is not None:
            *values, self.last = lax.optimization_barrier((*values, self.last))
        return values if len(values) > 1 else values[0]

    def done(self, *values):
        if self.last is not None:
            *values, _ = lax.optimization_barrier((*values, self.last))
        self.last = values[-1]
        return values if len(values) > 1 else values[0]


def exchange(first, second, project_next, send_hidden):
    half_z = NZ // 2 * SUB

    def column(dx, order):
        return [(0, dx, dz) for dz in order]

    def line(order, dz):
        return [(1, dx, dz) for dx in order]

    opposite = shift(first, 0, 4)
    left, right, far = shift(second, 1, 0), shift(second, -1, 0), shift(second, 2, 0)
    pair = jnp.concatenate([first, opposite], axis=0)
    up, down = shift(pair, 0, 1), shift(pair, 0, -1)
    row = jnp.concatenate([second, left, right, far], axis=0)
    up1, down1 = shift(row, 0, 1), shift(row, 0, -1)
    line_rows = NX * SUB
    (p_row,), (up, down) = project_next(
        [row], [(0, 0, line(X_ORDER, 0), 0, 0)], [line_rows], [], [up, down]
    )
    up_far, down_far = shift(up[:SUB], 0, 1), shift(down[:SUB], 0, -1)
    up2, down2 = shift(up1, 0, 1), shift(down1, 0, -1)
    col = jnp.concatenate([pair, up, down, up_far, down_far], axis=0)
    left, right = shift(col, 1, 0), shift(col, -1, 0)
    (p_up1, p_down1), (up2, down2) = project_next(
        [up1, down1],
        [(0, 0, line(X_ORDER, -1), 0, 0), (1, 0, line(X_ORDER, 1), 1, 0)],
        [line_rows] * 2,
        [],
        [up2, down2],
    )
    up3, down3 = shift(up2, 0, 1), shift(down2, 0, -1)
    (p_col, p_up2, p_down2), (left, right, up3, down3) = project_next(
        [col, up2, down2],
        [
            (0, 0, column(0, Z_ORDER), 0, 0),
            (1, 0, line(X_ORDER, -2), 1, 0),
            (2, 0, line(X_ORDER, 2), 2, 0),
        ],
        [2 * half_z, line_rows, line_rows],
        [],
        [left, right, up3, down3],
    )
    up4, down4 = shift(up3[: 2 * SUB], 0, 1), shift(down3[2 * SUB :], 0, -1)
    far_head, far_tail = shift(left[:half_z], 1, 0), shift(right[half_z:], -1, 0)
    heads, tails = Z_ORDER[: NZ // 2], Z_ORDER[NZ // 2 :]
    (to_right, to_left, p_left, p_right, p_up3, p_down3), (far_head, far_tail, up4, down4) = (
        project_next(
            [left, right, up3, down3],
            [
                (0, 0, column(-1, heads), 1, half_z),
                (0, half_z, column(-1, tails), 2, 0),
                (1, 0, column(1, heads), 3, 0),
                (1, half_z, column(1, tails), 0, half_z),
                (2, 0, line(X_ORDER, -3), 4, 0),
                (3, 0, line(X_ORDER, 3), 5, 0),
            ],
            [2 * half_z] * 2 + [half_z] * 2 + [line_rows] * 2,
            [],
            [far_head, far_tail, up4, down4],
        )
    )
    (to_right, to_left, p_up4, p_down4), _ = project_next(
        [far_head, far_tail, up4, down4],
        [
            (2, 0, line(X_ORDER[:2], 4), 2, 0),
            (3, 0, line(X_ORDER[2:], 4), 3, 0),
            (0, 0, column(2, heads), 0, 0),
            (1, 0, column(2, tails), 1, 0),
        ],
        [2 * half_z] * 2 + [2 * SUB] * 2,
        [to_right, to_left],
        [],
    )
    top, bottom = shift(p_up4, 0, -1), shift(p_down4, 0, 1)
    from_left, from_right = shift(to_right, 1, 0), shift(to_left, -1, 0)

    order = Order()
    p_up3 = jnp.concatenate([add(p_up3[: 2 * SUB], top), p_up3[2 * SUB :]], axis=0)
    p_down3 = jnp.concatenate([p_down3[: 2 * SUB], add(p_down3[2 * SUB :], bottom)], axis=0)
    p_up3, p_down3 = order.done(p_up3, p_down3)
    top, bottom = shift(p_up3, 0, -1), shift(p_down3, 0, 1)
    stream = send_hidden(order)
    p_up2, p_down2 = order.tie(p_up2, p_down2)
    p_up2, p_down2 = order.done(add(p_up2, top), add(p_down2, bottom))
    top, bottom = shift(p_up2, 0, -1), shift(p_down2, 0, 1)
    p_left, p_right = order.tie(p_left, p_right)
    p_right, p_left = order.done(
        add(p_right, from_left[:half_z]), add(p_left, from_right[:half_z])
    )
    from_left_head, from_right_tail = shift(p_right, 1, 0), shift(p_left, -1, 0)
    p_up1, p_down1 = order.tie(p_up1, p_down1)
    p_up1, p_down1 = order.done(add(p_up1, top), add(p_down1, bottom))
    top, bottom = shift(p_up1, 0, -1), shift(p_down1, 0, 1)
    p_col = order.tie(p_col)
    p_head, p_tail = order.done(
        add(p_col[:half_z], from_left_head, from_right[half_z:]),
        add(p_col[half_z:], from_left[half_z:], from_right_tail),
    )
    below = shift(p_tail[2 * SUB : 3 * SUB], 0, -1)
    above = shift(p_tail[3 * SUB :], 0, 1)
    p_row, stream = order.tie(p_row, stream)
    row = order.done(add(p_row, top, bottom))
    terms = [
        row[:SUB],
        shift(row[SUB : 2 * SUB], -1, 0),
        shift(row[2 * SUB : 3 * SUB], 1, 0),
        shift(row[3 * SUB :], 2, 0),
    ]
    p_head, p_tail = order.tie(p_head, p_tail)
    pair_down = jnp.concatenate(
        [add(p_head[2 * SUB : 3 * SUB], below), p_head[3 * SUB :]], axis=0
    )
    pair_up = jnp.concatenate([add(p_tail[:SUB], above), p_tail[SUB : 2 * SUB]], axis=0)
    pair_down, pair_up = order.done(pair_down, pair_up)
    from_above, from_below = shift(pair_down, 0, -1), shift(pair_up, 0, 1)
    pair = add(p_head[: 2 * SUB], from_above, from_below)
    first = pair[:SUB].astype(jnp.float32) + shift(pair[SUB:], 0, 4).astype(jnp.float32)
    second = sum(term.astype(jnp.float32) for term in terms)
    return jnp.concatenate([first, second], axis=0), stream


def body(projected, positions, out_weight, residual, norm_gain, next_weight):
    local_rows = projected[0]
    outer = lax.axis_index("outer")
    inner = lax.axis_index("inner")
    here = jnp.stack([outer % NX, inner * 2 + outer // NX])

    scaled = next_weight[0].astype(jnp.float32) * norm_gain[0].astype(jnp.float32)[:, None]
    weight_next = section_shift(scaled.astype(jnp.bfloat16), -1)

    first, second = attention(here, positions[::SUB], local_rows)
    hidden = []

    def project_next(chunks, pieces, part_rows, started, held):
        outs, parts = project(
            here,
            (out_weight[0], weight_next),
            residual[0],
            hidden,
            chunks,
            pieces,
            part_rows,
            started,
        )
        if held:
            outs[0], held = lax.optimization_barrier((outs[0], held))
        hidden[:] = outs
        return parts, held

    def send_hidden(order):
        return section_shift(order.tie(hidden[0])[None], 1)

    summed, stream = exchange(first, second, project_next, send_hidden)
    inverse_rms = lax.rsqrt(summed[:, QW : QW + 1] / D + 1e-05)
    result = (summed[:, :QW] * inverse_rms).astype(jnp.bfloat16)
    return (section_shift(result[None], 1), stream)


def solution(mesh):
    return jax.shard_map(
        body,
        mesh=mesh,
        in_specs=(
            P("section", ("outer", "inner"), None),
            P(),
            P("section", None, ("outer", "inner")),
            P("section", None, ("outer", "inner")),
            P("section", ("outer", "inner")),
            P("section", ("outer", "inner"), None),
        ),
        out_specs=(P("section", ("outer", "inner"), None), P("section", None, ("outer", "inner"))),
        check_vma=False,
    )
```

```python
import functools

import jax
import jax.numpy as jnp
from jax import lax
from jax.experimental import pallas as pl
from jax.experimental.pallas import tpu as pltpu
from jax.sharding import PartitionSpec as P

D = 16384
HQ = 8
HD = 128
QW = 1280
SUB = 64
PW = QW + 128
NX = 4
NZ = 8
SHARD_AXES = ("outer", "inner")
Z_ORDER = (0, -1, 4, 1, -2, 3, -3, 2)
X_ORDER = (0, -1, 1, 2)
KEY_BLOCK = 256
VMEM_GRANT = 12 * 1024 * 1024


def shard_of(x, z):
    x = x & (NX - 1)
    z = z & (NZ - 1)
    return (z & 1) * 16 + x * 4 + (z >> 1)


def run_of(here, half, dx, dz):
    return shard_of(here[0] + dx, here[1] + dz) * 2 + half


def shift(value, dx, dz):
    pairs = [
        (shard_of(x, z), shard_of(x + dx, z + dz)) for x in range(NX) for z in range(NZ)
    ]
    return lax.ppermute(value, SHARD_AXES, pairs)


def section_shift(value, by):
    return lax.ppermute(value, "section", [(i, (i + by) % 8) for i in range(8)])


def attend_kernel(sizes, runs, is_first, is_last, here, run_starts, *refs):
    count = len(sizes)
    rows = refs[0]
    chunks = refs[1 : count + 1]
    refs = refs[count + 1 :]
    tokens = rows.shape[0]
    columns = HQ * tokens
    if is_first:
        largest = jnp.full((1, columns), -1e30, jnp.float32)
        total = jnp.zeros((1, columns), jnp.float32)
        acc = jnp.zeros((HD, columns), jnp.float32)
    else:
        largest, total, acc = refs[0][...], refs[1][...], refs[2][...]
        refs = refs[3:]
    stacked = jnp.concatenate([rows[:, h * HD : (h + 1) * HD] for h in range(HQ)], axis=0)
    lane = lax.broadcasted_iota(jnp.int32, (1, tokens), 1)
    query_positions = lane
    for run in range(tokens // SUB):
        start = run_starts[run_of(here, run, 0, 0)] - run * SUB
        query_positions = jnp.where(lane // SUB == run, lane + start, query_positions)
    row_index = lax.broadcasted_iota(jnp.int32, (SUB, tokens), 0)
    factor = HD ** (-0.5) * 1.4426950408889634
    run = 0
    for chunk, size in zip(chunks, sizes):
        for start in range(0, size, KEY_BLOCK):
            keys = chunk[pl.ds(start, KEY_BLOCK), :HD]
            values = chunk[pl.ds(start, KEY_BLOCK), HD:]
            scores = lax.dot_general(
                keys, stacked, (((1,), (1,)), ((), ())), preferred_element_type=jnp.float32
            )
            masked = []
            for part in range(KEY_BLOCK // SUB):
                start_here = run_starts[run_of(here, *runs[run])]
                visible = row_index + start_here <= query_positions
                visible = jnp.concatenate([visible] * HQ, axis=1)
                block = scores[part * SUB : (part + 1) * SUB] * factor
                masked.append(jnp.where(visible, block, -jnp.inf))
                run += 1
            masked = jnp.concatenate(masked, axis=0)
            new_largest = jnp.maximum(largest, jnp.max(masked, axis=0, keepdims=True))
            weights = jnp.exp2(masked - new_largest)
            keep = jnp.exp2(largest - new_largest)
            total = total * keep + jnp.sum(weights, axis=0, keepdims=True)
            acc = acc * keep + lax.dot_general(
                values,
                weights.astype(jnp.bfloat16),
                (((0,), (0,)), ((), ())),
                preferred_element_type=jnp.float32,
            )
            largest = new_largest
    if is_last:
        mixed = acc / total
        for h in range(HQ):
            turned = jnp.transpose(mixed[:, h * tokens : (h + 1) * tokens]).astype(jnp.bfloat16)
            for half in range(2):
                refs[half][:, h * HD : (h + 1) * HD] = turned[half * SUB : (half + 1) * SUB]
    else:
        refs[0][...], refs[1][...], refs[2][...] = largest, total, acc


def attend(here, run_starts, rows, chunks, runs, state, is_last=False):
    sizes = [chunk.shape[0] for chunk in chunks]
    columns = HQ * rows.shape[0]
    smem = pl.BlockSpec(memory_space=pltpu.SMEM)
    vmem = pl.BlockSpec(memory_space=pltpu.VMEM)
    if is_last:
        out_shape = [jax.ShapeDtypeStruct((SUB, HQ * HD), jnp.bfloat16)] * 2
    else:
        out_shape = [
            jax.ShapeDtypeStruct((1, columns), jnp.float32),
            jax.ShapeDtypeStruct((1, columns), jnp.float32),
            jax.ShapeDtypeStruct((HD, columns), jnp.float32),
        ]
    return pl.pallas_call(
        functools.partial(attend_kernel, sizes, runs, not state, is_last),
        out_shape=out_shape,
        in_specs=[smem, smem] + [vmem] * (1 + len(chunks) + len(state)),
        out_specs=[vmem] * len(out_shape),
        compiler_params=pltpu.CompilerParams(vmem_limit_bytes=16 * 1024 * 1024),
        cost_estimate=pl.CostEstimate(
            flops=8 * sum(sizes) * columns * HD,
            bytes_accessed=4 * columns * HD,
            transcendentals=sum(sizes) * columns,
        ),
    )(here, run_starts, rows, *chunks, *state)


def nearest(value):
    return value, shift(value, 0, 1), shift(value, 0, 4), shift(value, 0, -1)


def farther(quad):
    rows = quad.shape[0] // 4
    return shift(quad[rows : 3 * rows], 0, 1), shift(quad[2 * rows :], 0, -1)


def attention(here, run_starts, rows, weight_next):
    quad = jnp.concatenate(nearest(rows[:, HQ * HD :]), axis=0)
    col = jnp.concatenate([quad, *farther(quad)], axis=0)
    half = col.shape[0] // 2
    step = functools.partial(attend, here, run_starts, rows)

    def column(dx, order=Z_ORDER):
        return [(part, dx, dz) for dz in order for part in range(2)]

    left, right = shift(col, 1, 0), shift(col, -1, 0)
    state = step([col], column(0), [])
    left, right, state = lax.optimization_barrier((left, right, state))
    far_head, far_tail = shift(left[:half], 1, 0), shift(right[half:], -1, 0)
    state = step([left, right], column(-1) + column(1), state)
    far_head, far_tail, state, weight_next = lax.optimization_barrier(
        (far_head, far_tail, state, weight_next)
    )
    runs = column(2, Z_ORDER[: NZ // 2]) + column(2, Z_ORDER[NZ // 2 :])
    return step([far_head, far_tail], runs, state, True), weight_next


def add(*terms):
    total = terms[0].astype(jnp.float32)
    for term in terms[1:]:
        total = total + term.astype(jnp.float32)
    return total.astype(jnp.bfloat16)


def project_kernel(pieces, kept, here, *refs):
    weight_out, residual, weight_next = refs[:3]
    chunks = refs[3 : 3 + len({piece[0] for piece in pieces})]
    outs = refs[3 + len(chunks) + kept :]
    hidden, parts = outs[0], outs[1:]
    for chunk, start, runs, part, part_start in pieces:
        size = len(runs) * SUB
        product = jnp.dot(
            chunks[chunk][pl.ds(start, size)], weight_out[...], preferred_element_type=jnp.float32
        )
        rows = []
        for sub, run in enumerate(runs):
            offset = pl.multiple_of(run_of(here, *run) * SUB, SUB)
            sums = residual[pl.ds(offset, SUB)].astype(jnp.float32)
            sums = (sums + product[sub * SUB : (sub + 1) * SUB]).astype(jnp.bfloat16)
            hidden[pl.ds(offset, SUB)] = sums
            rows.append(sums)
        rows = jnp.concatenate(rows, axis=0)
        place = pl.ds(part_start, size)
        parts[part][place, :QW] = jnp.dot(
            rows, weight_next[...], preferred_element_type=jnp.float32
        ).astype(jnp.bfloat16)
        wide = rows.astype(jnp.float32)
        squares = jnp.sum(wide * wide, axis=1, keepdims=True)
        parts[part][place, QW:] = jnp.broadcast_to(squares, (size, PW - QW)).astype(jnp.bfloat16)


def project(here, weights, residual, hidden, chunks, pieces, part_rows, started=()):
    total = sum(len(piece[2]) for piece in pieces) * SUB
    width = residual.shape[1]
    kept = [*hidden, *started]
    vmem = pl.BlockSpec(memory_space=pltpu.VMEM)
    hidden, *parts = pl.pallas_call(
        functools.partial(project_kernel, pieces, len(kept)),
        out_shape=[jax.ShapeDtypeStruct(residual.shape, residual.dtype)]
        + [jax.ShapeDtypeStruct((rows, PW), jnp.bfloat16) for rows in part_rows],
        in_specs=[pl.BlockSpec(memory_space=pltpu.SMEM)]
        + [vmem] * (3 + len(chunks) + len(kept)),
        out_specs=[vmem] * (1 + len(part_rows)),
        input_output_aliases={4 + len(chunks) + i: i for i in range(len(kept))},
        compiler_params=pltpu.CompilerParams(vmem_limit_bytes=VMEM_GRANT),
        cost_estimate=pl.CostEstimate(
            flops=2 * total * width * (HQ * HD + QW),
            bytes_accessed=2 * total * (HQ * HD + 2 * width + PW) + 2 * width * (HQ * HD + QW),
            transcendentals=0,
        ),
    )(here, weights[0], residual, weights[1], *chunks, *kept)
    return [hidden], parts


def copy_kernel(source, target):
    target[...] = source[...]


def in_hbm(value):
    block = pl.BlockSpec((1, 512, value.shape[2]), lambda i: (0, i, 0))
    return pl.pallas_call(
        copy_kernel,
        grid=(value.shape[1] // 512,),
        out_shape=jax.ShapeDtypeStruct(value.shape, value.dtype),
        in_specs=[block],
        out_specs=block,
        cost_estimate=pl.CostEstimate(
            flops=0, bytes_accessed=4 * value.size, transcendentals=0
        ),
    )(value)


class Order:
    def __init__(self):
        self.last = None

    def tie(self, *values):
        if self.last is not None:
            *values, self.last = lax.optimization_barrier((*values, self.last))
        return values if len(values) > 1 else values[0]

    def done(self, *values):
        if self.last is not None:
            *values, _ = lax.optimization_barrier((*values, self.last))
        self.last = values[-1]
        return values if len(values) > 1 else values[0]


def exchange(first, second, project_next, send_hidden):
    half_z = NZ // 2 * SUB

    def column(dx, order):
        return [(0, dx, dz) for dz in order]

    def line(order, dz):
        return [(1, dx, dz) for dx in order]

    quad = nearest(first)
    row = second, shift(second, 1, 0), shift(second, -1, 0), shift(second, 2, 0)
    quad, row = lax.optimization_barrier((quad, row))
    quad, row = lax.optimization_barrier((jnp.concatenate(quad, axis=0), row))
    row = jnp.concatenate(row, axis=0)
    up_rest, down_rest = farther(quad)
    up1, down1 = shift(row, 0, 1), shift(row, 0, -1)
    line_rows = NX * SUB
    (p_row,), (up_rest, down_rest) = project_next(
        [row], [(0, 0, line(X_ORDER, 0), 0, 0)], [line_rows], [], [up_rest, down_rest]
    )
    col = jnp.concatenate([quad, up_rest, down_rest], axis=0)
    left, right = shift(col, 1, 0), shift(col, -1, 0)
    up2, down2 = shift(up1, 0, 1), shift(down1, 0, -1)
    (p_up1, p_down1), (up2, down2) = project_next(
        [up1, down1],
        [(0, 0, line(X_ORDER, -1), 0, 0), (1, 0, line(X_ORDER, 1), 1, 0)],
        [line_rows] * 2,
        [],
        [up2, down2],
    )
    up3, down3 = shift(up2, 0, 1), shift(down2, 0, -1)
    (p_col, p_up2, p_down2), (left, right, up3, down3) = project_next(
        [col, up2, down2],
        [
            (0, 0, column(0, Z_ORDER), 0, 0),
            (1, 0, line(X_ORDER, -2), 1, 0),
            (2, 0, line(X_ORDER, 2), 2, 0),
        ],
        [2 * half_z, line_rows, line_rows],
        [],
        [left, right, up3, down3],
    )
    up4, down4 = shift(up3[: 2 * SUB], 0, 1), shift(down3[2 * SUB :], 0, -1)
    far_head, far_tail = shift(left[:half_z], 1, 0), shift(right[half_z:], -1, 0)
    heads, tails = Z_ORDER[: NZ // 2], Z_ORDER[NZ // 2 :]
    (to_right, to_left, p_left, p_right, p_up3, p_down3), (far_head, far_tail, up4, down4) = (
        project_next(
            [left, right, up3, down3],
            [
                (0, 0, column(-1, heads), 1, half_z),
                (0, half_z, column(-1, tails), 2, 0),
                (1, 0, column(1, heads), 3, 0),
                (1, half_z, column(1, tails), 0, half_z),
                (2, 0, line(X_ORDER, -3), 4, 0),
                (3, 0, line(X_ORDER, 3), 5, 0),
            ],
            [2 * half_z] * 2 + [half_z] * 2 + [line_rows] * 2,
            [],
            [far_head, far_tail, up4, down4],
        )
    )
    (to_right, to_left, p_up4, p_down4), _ = project_next(
        [far_head, far_tail, up4, down4],
        [
            (2, 0, line(X_ORDER[:2], 4), 2, 0),
            (3, 0, line(X_ORDER[2:], 4), 3, 0),
            (0, 0, column(2, heads), 0, 0),
            (1, 0, column(2, tails), 1, 0),
        ],
        [2 * half_z] * 2 + [2 * SUB] * 2,
        [to_right, to_left],
        [],
    )
    top, bottom = shift(p_up4, 0, -1), shift(p_down4, 0, 1)
    from_left, from_right = shift(to_right, 1, 0), shift(to_left, -1, 0)

    order = Order()
    p_up3 = jnp.concatenate([add(p_up3[: 2 * SUB], top), p_up3[2 * SUB :]], axis=0)
    p_down3 = jnp.concatenate([p_down3[: 2 * SUB], add(p_down3[2 * SUB :], bottom)], axis=0)
    p_up3, p_down3 = order.done(p_up3, p_down3)
    top, bottom = shift(p_up3, 0, -1), shift(p_down3, 0, 1)
    stream = send_hidden(order)
    p_up2, p_down2 = order.tie(p_up2, p_down2)
    p_up2, p_down2 = order.done(add(p_up2, top), add(p_down2, bottom))
    top, bottom = shift(p_up2, 0, -1), shift(p_down2, 0, 1)
    p_left, p_right = order.tie(p_left, p_right)
    p_right, p_left = order.done(
        add(p_right, from_left[:half_z]), add(p_left, from_right[:half_z])
    )
    from_left_head, from_right_tail = shift(p_right, 1, 0), shift(p_left, -1, 0)
    p_up1, p_down1 = order.tie(p_up1, p_down1)
    p_up1, p_down1 = order.done(add(p_up1, top), add(p_down1, bottom))
    top, bottom = shift(p_up1, 0, -1), shift(p_down1, 0, 1)
    p_col = order.tie(p_col)
    p_head, p_tail = order.done(
        add(p_col[:half_z], from_left_head, from_right[half_z:]),
        add(p_col[half_z:], from_left[half_z:], from_right_tail),
    )
    from_above = shift(p_tail[: 2 * SUB], 0, -1)
    from_below = shift(p_tail[2 * SUB :], 0, 1)
    p_row, stream = order.tie(p_row, stream)
    row = order.done(add(p_row, top, bottom))
    terms = [
        row[:SUB],
        shift(row[SUB : 2 * SUB], -1, 0),
        shift(row[2 * SUB : 3 * SUB], 1, 0),
        shift(row[3 * SUB :], 2, 0),
    ]
    p_head = order.tie(p_head)
    behind = add(p_head[SUB : 2 * SUB], from_above[:SUB])
    opposite = add(p_head[2 * SUB : 3 * SUB], from_above[SUB:], from_below[:SUB])
    ahead = add(p_head[3 * SUB :], from_below[SUB:])
    others = [p_head[:SUB], shift(behind, 0, -1), shift(opposite, 0, 4), shift(ahead, 0, 1)]
    first = sum(term.astype(jnp.float32) for term in others)
    second = sum(term.astype(jnp.float32) for term in terms)
    return jnp.concatenate([first, second], axis=0), stream


def body(projected, positions, out_weight, residual, norm_gain, next_weight):
    local_rows = projected[0]
    outer = lax.axis_index("outer")
    inner = lax.axis_index("inner")
    here = jnp.stack([outer % NX, inner * 2 + outer // NX])

    scaled = next_weight[0].astype(jnp.float32) * norm_gain[0].astype(jnp.float32)[:, None]
    weight_next = section_shift(scaled.astype(jnp.bfloat16), -1)

    (first, second), weight_next = attention(here, positions[::SUB], local_rows, weight_next)
    hidden = []

    def project_next(chunks, pieces, part_rows, started, held):
        outs, parts = project(
            here,
            (out_weight[0], weight_next),
            residual[0],
            hidden,
            chunks,
            pieces,
            part_rows,
            started,
        )
        if held:
            outs[0], held = lax.optimization_barrier((outs[0], held))
        hidden[:] = outs
        return parts, held

    def send_hidden(order):
        return section_shift(order.tie(hidden[0])[None], 1)

    summed, stream = exchange(first, second, project_next, send_hidden)
    inverse_rms = lax.rsqrt(summed[:, QW : QW + 1] / D + 1e-05)
    result = (summed[:, :QW] * inverse_rms).astype(jnp.bfloat16)
    return (section_shift(result[None], 1), in_hbm(stream))


def solution(mesh):
    return jax.shard_map(
        body,
        mesh=mesh,
        in_specs=(
            P("section", ("outer", "inner"), None),
            P(),
            P("section", None, ("outer", "inner")),
            P("section", None, ("outer", "inner")),
            P("section", ("outer", "inner")),
            P("section", ("outer", "inner"), None),
        ),
        out_specs=(P("section", ("outer", "inner"), None), P("section", None, ("outer", "inner"))),
        check_vma=False,
    )
```

```python
import functools

import jax
import jax.numpy as jnp
from jax import lax
from jax.experimental import pallas as pl
from jax.experimental.pallas import tpu as pltpu
from jax.sharding import PartitionSpec as P

D = 16384
HQ = 8
HD = 128
QW = 1280
SUB = 64
PW = QW + 128
NX = 4
NZ = 8
SHARD_AXES = ("outer", "inner")
QUAD = (0, -1, 4, 1)
REST = (-2, 3, -3, 2)
X_ORDER = (0, -1, 1, 2)
KEY_BLOCK = 256
SHARES = (80, 48)
VMEM_GRANT = 12 * 1024 * 1024


def shard_of(x, z):
    x = x & (NX - 1)
    z = z & (NZ - 1)
    return (z & 1) * 16 + x * 4 + (z >> 1)


def run_of(here, half, dx, dz):
    return shard_of(here[0] + dx, here[1] + dz) * 2 + half


def shift(value, dx, dz):
    pairs = [
        (shard_of(x, z), shard_of(x + dx, z + dz)) for x in range(NX) for z in range(NZ)
    ]
    return lax.ppermute(value, SHARD_AXES, pairs)


def section_shift(value, by):
    return lax.ppermute(value, "section", [(i, (i + by) % 8) for i in range(8)])


def attend_kernel(sizes, runs, is_first, is_last, here, run_starts, *refs):
    count = len(sizes)
    rows = refs[0]
    chunks = refs[1 : count + 1]
    refs = refs[count + 1 :]
    tokens = rows.shape[0]
    columns = HQ * tokens
    if is_first:
        largest = jnp.full((1, columns), -1e30, jnp.float32)
        total = jnp.zeros((1, columns), jnp.float32)
        acc = jnp.zeros((HD, columns), jnp.float32)
    else:
        largest, total, acc = refs[0][...], refs[1][...], refs[2][...]
        refs = refs[3:]
    stacked = jnp.concatenate([rows[:, h * HD : (h + 1) * HD] for h in range(HQ)], axis=0)
    lane = lax.broadcasted_iota(jnp.int32, (1, tokens), 1)
    query_positions = lane
    for run in range(tokens // SUB):
        start = run_starts[run_of(here, run, 0, 0)] - run * SUB
        query_positions = jnp.where(lane // SUB == run, lane + start, query_positions)
    row_index = lax.broadcasted_iota(jnp.int32, (SUB, tokens), 0)
    factor = HD ** (-0.5) * 1.4426950408889634
    run = 0
    for chunk, size in zip(chunks, sizes):
        for start in range(0, size, KEY_BLOCK):
            keys = chunk[pl.ds(start, KEY_BLOCK), :HD]
            values = chunk[pl.ds(start, KEY_BLOCK), HD:]
            scores = lax.dot_general(
                keys, stacked, (((1,), (1,)), ((), ())), preferred_element_type=jnp.float32
            )
            masked = []
            for part in range(KEY_BLOCK // SUB):
                start_here = run_starts[run_of(here, *runs[run])]
                visible = row_index + start_here <= query_positions
                visible = jnp.concatenate([visible] * HQ, axis=1)
                block = scores[part * SUB : (part + 1) * SUB] * factor
                masked.append(jnp.where(visible, block, -jnp.inf))
                run += 1
            masked = jnp.concatenate(masked, axis=0)
            new_largest = jnp.maximum(largest, jnp.max(masked, axis=0, keepdims=True))
            weights = jnp.exp2(masked - new_largest)
            keep = jnp.exp2(largest - new_largest)
            total = total * keep + jnp.sum(weights, axis=0, keepdims=True)
            acc = acc * keep + lax.dot_general(
                values,
                weights.astype(jnp.bfloat16),
                (((0,), (0,)), ((), ())),
                preferred_element_type=jnp.float32,
            )
            largest = new_largest
    if is_last:
        mixed = acc / total
        for h in range(HQ):
            turned = jnp.transpose(mixed[:, h * tokens : (h + 1) * tokens]).astype(jnp.bfloat16)
            refs[0][:, h * HD : (h + 1) * HD] = turned[: SHARES[0]]
            refs[1][:, h * HD : (h + 1) * HD] = turned[SHARES[0] :]
    else:
        refs[0][...], refs[1][...], refs[2][...] = largest, total, acc


def attend(here, run_starts, rows, chunks, runs, state, is_last=False):
    sizes = [chunk.shape[0] for chunk in chunks]
    columns = HQ * rows.shape[0]
    smem = pl.BlockSpec(memory_space=pltpu.SMEM)
    vmem = pl.BlockSpec(memory_space=pltpu.VMEM)
    if is_last:
        out_shape = [jax.ShapeDtypeStruct((share, HQ * HD), jnp.bfloat16) for share in SHARES]
    else:
        out_shape = [
            jax.ShapeDtypeStruct((1, columns), jnp.float32),
            jax.ShapeDtypeStruct((1, columns), jnp.float32),
            jax.ShapeDtypeStruct((HD, columns), jnp.float32),
        ]
    return pl.pallas_call(
        functools.partial(attend_kernel, sizes, runs, not state, is_last),
        out_shape=out_shape,
        in_specs=[smem, smem] + [vmem] * (1 + len(chunks) + len(state)),
        out_specs=[vmem] * len(out_shape),
        compiler_params=pltpu.CompilerParams(vmem_limit_bytes=16 * 1024 * 1024),
        cost_estimate=pl.CostEstimate(
            flops=8 * sum(sizes) * columns * HD,
            bytes_accessed=4 * columns * HD,
            transcendentals=sum(sizes) * columns,
        ),
    )(here, run_starts, rows, *chunks, *state)


def nearest(value):
    return value, shift(value, 0, 1), shift(value, 0, 4), shift(value, 0, -1)


def farther(quad):
    rows = quad.shape[0] // 4
    return shift(quad[rows : 3 * rows], 0, 1), shift(quad[2 * rows :], 0, -1)


def attention(here, run_starts, rows, send_weight):
    quad = jnp.concatenate(nearest(rows[:, HQ * HD :]), axis=0)
    step = functools.partial(attend, here, run_starts, rows)

    def column(dx, order):
        return [(part, dx, dz) for dz in order for part in range(2)]

    quad, weight_next = send_weight(quad)
    rest = farther(quad)
    left_quad, right_quad = shift(quad, 1, 0), shift(quad, -1, 0)
    state = step([quad], column(0, QUAD), [])
    rest, state = lax.optimization_barrier((jnp.concatenate(rest, axis=0), state))
    left_rest, right_rest = shift(rest, 1, 0), shift(rest, -1, 0)
    far_quad = shift(left_quad, 1, 0)
    state = step(
        [left_quad, right_quad, rest], column(-1, QUAD) + column(1, QUAD) + column(0, REST), state
    )
    right_rest, state = lax.optimization_barrier((right_rest, state))
    far_rest = shift(right_rest, -1, 0)
    runs = column(-1, REST) + column(1, REST) + column(2, QUAD)
    state = step([left_rest, right_rest, far_quad], runs, state)
    state, weight_next = lax.optimization_barrier((state, weight_next))
    return step([far_rest], column(2, REST), state, True), weight_next


def add(*terms):
    total = terms[0].astype(jnp.float32)
    for term in terms[1:]:
        total = total + term.astype(jnp.float32)
    return total.astype(jnp.bfloat16)


def project_kernel(pieces, kept, here, *refs):
    weight_out, residual, weight_next = refs[:3]
    chunks = refs[3 : 3 + len({piece[0] for piece in pieces})]
    outs = refs[3 + len(chunks) + kept :]
    hidden, parts = outs[0], outs[1:]
    for chunk, start, runs, part, part_start in pieces:
        share = SHARES[runs[0][0]]
        size = len(runs) * share
        product = jnp.dot(
            chunks[chunk][pl.ds(start, size)], weight_out[...], preferred_element_type=jnp.float32
        )
        rows = []
        for sub, run in enumerate(runs):
            shard = shard_of(here[0] + run[1], here[1] + run[2])
            offset = pl.multiple_of(shard * sum(SHARES) + run[0] * SHARES[0], 16)
            sums = residual[pl.ds(offset, share)].astype(jnp.float32)
            sums = (sums + product[sub * share : (sub + 1) * share]).astype(jnp.bfloat16)
            hidden[pl.ds(offset, share)] = sums
            rows.append(sums)
        rows = jnp.concatenate(rows, axis=0)
        place = pl.ds(part_start, size)
        parts[part][place, :QW] = jnp.dot(
            rows, weight_next[...], preferred_element_type=jnp.float32
        ).astype(jnp.bfloat16)
        wide = rows.astype(jnp.float32)
        squares = jnp.sum(wide * wide, axis=1, keepdims=True)
        parts[part][place, QW:] = jnp.broadcast_to(squares, (size, PW - QW)).astype(jnp.bfloat16)


def project(here, weights, residual, hidden, chunks, pieces, part_rows, started=()):
    total = sum(chunk.shape[0] for chunk in chunks)
    width = residual.shape[1]
    kept = [*hidden, *started]
    vmem = pl.BlockSpec(memory_space=pltpu.VMEM)
    hidden, *parts = pl.pallas_call(
        functools.partial(project_kernel, pieces, len(kept)),
        out_shape=[jax.ShapeDtypeStruct(residual.shape, residual.dtype)]
        + [jax.ShapeDtypeStruct((rows, PW), jnp.bfloat16) for rows in part_rows],
        in_specs=[pl.BlockSpec(memory_space=pltpu.SMEM)]
        + [vmem] * (3 + len(chunks) + len(kept)),
        out_specs=[vmem] * (1 + len(part_rows)),
        input_output_aliases={4 + len(chunks) + i: i for i in range(len(kept))},
        compiler_params=pltpu.CompilerParams(vmem_limit_bytes=VMEM_GRANT),
        cost_estimate=pl.CostEstimate(
            flops=2 * total * width * (HQ * HD + QW),
            bytes_accessed=2 * total * (HQ * HD + 2 * width + PW) + 2 * width * (HQ * HD + QW),
            transcendentals=0,
        ),
    )(here, weights[0], residual, weights[1], *chunks, *kept)
    return [hidden], parts


def copy_kernel(source, target):
    target[...] = source[...]


def in_hbm(value):
    block = pl.BlockSpec((1, 512, value.shape[2]), lambda i: (0, i, 0))
    return pl.pallas_call(
        copy_kernel,
        grid=(value.shape[1] // 512,),
        out_shape=jax.ShapeDtypeStruct(value.shape, value.dtype),
        in_specs=[block],
        out_specs=block,
        cost_estimate=pl.CostEstimate(
            flops=0, bytes_accessed=4 * value.size, transcendentals=0
        ),
    )(value)


class Order:
    def __init__(self):
        self.last = None

    def tie(self, *values):
        if self.last is not None:
            *values, self.last = lax.optimization_barrier((*values, self.last))
        return values if len(values) > 1 else values[0]

    def done(self, *values):
        if self.last is not None:
            *values, _ = lax.optimization_barrier((*values, self.last))
        self.last = values[-1]
        return values if len(values) > 1 else values[0]


def exchange(first, second, project_next, send_hidden):
    quad_rows, line_rows = 4 * SHARES[0], NX * SHARES[1]

    def column(dx, order):
        return [(0, dx, dz) for dz in order]

    def line(order, dz):
        return [(1, dx, dz) for dx in order]

    quad = nearest(first)
    row = second, shift(second, 1, 0), shift(second, -1, 0), shift(second, 2, 0)
    quad, row = lax.optimization_barrier((quad, row))
    quad, row = lax.optimization_barrier((jnp.concatenate(quad, axis=0), row))
    row = jnp.concatenate(row, axis=0)
    up_rest, down_rest = farther(quad)
    up1, down1 = shift(row, 0, 1), shift(row, 0, -1)
    left_quad, right_quad = shift(quad, 1, 0), shift(quad, -1, 0)
    (p_row, p_head), (up_rest, down_rest) = project_next(
        [row, quad],
        [(0, 0, line(X_ORDER, 0), 0, 0), (1, 0, column(0, QUAD), 1, 0)],
        [line_rows, quad_rows],
        [],
        [up_rest, down_rest],
    )
    rest = jnp.concatenate([up_rest, down_rest], axis=0)
    left_rest, right_rest = shift(rest, 1, 0), shift(rest, -1, 0)
    up2, down2 = shift(up1, 0, 1), shift(down1, 0, -1)
    (p_up1, p_down1), (left_quad, right_quad) = project_next(
        [up1, down1],
        [(0, 0, line(X_ORDER, -1), 0, 0), (1, 0, line(X_ORDER, 1), 1, 0)],
        [line_rows] * 2,
        [],
        [left_quad, right_quad],
    )
    far_quad = shift(left_quad, 1, 0)
    (to_left, p_right_head, p_tail), (up2, down2) = project_next(
        [left_quad, right_quad, rest],
        [
            (0, 0, column(-1, QUAD), 0, quad_rows),
            (1, 0, column(1, QUAD), 1, 0),
            (2, 0, column(0, REST), 2, 0),
        ],
        [2 * quad_rows, quad_rows, quad_rows],
        [],
        [up2, down2],
    )
    up3, down3 = shift(up2, 0, 1), shift(down2, 0, -1)
    (p_up2, p_down2), (left_rest, right_rest) = project_next(
        [up2, down2],
        [(0, 0, line(X_ORDER, -2), 0, 0), (1, 0, line(X_ORDER, 2), 1, 0)],
        [line_rows] * 2,
        [],
        [left_rest, right_rest],
    )
    far_rest = shift(right_rest, -1, 0)
    (to_right, p_left_tail), (up3, down3) = project_next(
        [far_quad, left_rest, right_rest],
        [
            (0, 0, column(2, QUAD), 0, 0),
            (1, 0, column(-1, REST), 1, 0),
            (2, 0, column(1, REST), 0, quad_rows),
        ],
        [2 * quad_rows, quad_rows],
        [],
        [up3, down3],
    )
    from_left = shift(to_right, 1, 0)
    up4, down4 = shift(up3[: line_rows // 2], 0, 1), shift(down3[line_rows // 2 :], 0, -1)
    (to_left, p_up3, p_down3), (up4, down4) = project_next(
        [far_rest, up3, down3],
        [
            (0, 0, column(2, REST), 0, 0),
            (1, 0, line(X_ORDER, -3), 1, 0),
            (2, 0, line(X_ORDER, 3), 2, 0),
        ],
        [2 * quad_rows, line_rows, line_rows],
        [to_left],
        [up4, down4],
    )
    from_right = shift(to_left, -1, 0)
    (p_up4, p_down4), _ = project_next(
        [up4, down4],
        [(0, 0, line(X_ORDER[:2], 4), 0, 0), (1, 0, line(X_ORDER[2:], 4), 1, 0)],
        [line_rows // 2] * 2,
        [],
        [],
    )
    top, bottom = shift(p_up4, 0, -1), shift(p_down4, 0, 1)

    order = Order()
    cut = line_rows // 2
    p_up3 = jnp.concatenate([add(p_up3[:cut], top), p_up3[cut:]], axis=0)
    p_down3 = jnp.concatenate([p_down3[:cut], add(p_down3[cut:], bottom)], axis=0)
    p_up3, p_down3 = order.done(p_up3, p_down3)
    top, bottom = shift(p_up3, 0, -1), shift(p_down3, 0, 1)
    stream = send_hidden(order)
    p_right_head, p_left_tail = order.tie(p_right_head, p_left_tail)
    p_right_head, p_left_tail = order.done(
        add(p_right_head, from_left[:quad_rows]), add(p_left_tail, from_right[:quad_rows])
    )
    from_left_head, from_right_tail = shift(p_right_head, 1, 0), shift(p_left_tail, -1, 0)
    p_up2, p_down2 = order.tie(p_up2, p_down2)
    p_up2, p_down2 = order.done(add(p_up2, top), add(p_down2, bottom))
    top, bottom = shift(p_up2, 0, -1), shift(p_down2, 0, 1)
    p_up1, p_down1 = order.tie(p_up1, p_down1)
    p_up1, p_down1 = order.done(add(p_up1, top), add(p_down1, bottom))
    top, bottom = shift(p_up1, 0, -1), shift(p_down1, 0, 1)
    p_head, p_tail = order.tie(p_head, p_tail)
    p_head, p_tail = order.done(
        add(p_head, from_left_head, from_right[quad_rows:]),
        add(p_tail, from_left[quad_rows:], from_right_tail),
    )
    share = SHARES[0]
    from_above = shift(p_tail[: 2 * share], 0, -1)
    from_below = shift(p_tail[2 * share :], 0, 1)
    p_row, stream = order.tie(p_row, stream)
    row = order.done(add(p_row, top, bottom))
    share = SHARES[1]
    terms = [
        row[:share],
        shift(row[share : 2 * share], -1, 0),
        shift(row[2 * share : 3 * share], 1, 0),
        shift(row[3 * share :], 2, 0),
    ]
    p_head = order.tie(p_head)
    share = SHARES[0]
    behind = add(p_head[share : 2 * share], from_above[:share])
    opposite = add(p_head[2 * share : 3 * share], from_above[share:], from_below[:share])
    ahead = add(p_head[3 * share :], from_below[share:])
    others = [shift(opposite, 0, 4), p_head[:share], shift(behind, 0, -1), shift(ahead, 0, 1)]
    first = sum(term.astype(jnp.float32) for term in others)
    second = sum(term.astype(jnp.float32) for term in terms)
    return jnp.concatenate([first, second], axis=0), stream


def body(projected, positions, out_weight, residual, norm_gain, next_weight):
    local_rows = projected[0]
    outer = lax.axis_index("outer")
    inner = lax.axis_index("inner")
    here = jnp.stack([outer % NX, inner * 2 + outer // NX])

    def send_weight(quad):
        quad, weight = lax.optimization_barrier((quad, next_weight[0]))
        scaled = weight.astype(jnp.float32) * norm_gain[0].astype(jnp.float32)[:, None]
        return quad, section_shift(scaled.astype(jnp.bfloat16), -1)

    (first, second), weight_next = attention(
        here, positions[::SUB], local_rows, send_weight
    )
    hidden = []

    def project_next(chunks, pieces, part_rows, started, held):
        outs, parts = project(
            here,
            (out_weight[0], weight_next),
            residual[0],
            hidden,
            chunks,
            pieces,
            part_rows,
            started,
        )
        if held:
            outs[0], held = lax.optimization_barrier((outs[0], held))
        hidden[:] = outs
        return parts, held

    def send_hidden(order):
        return section_shift(order.tie(hidden[0])[None], 1)

    summed, stream = exchange(first, second, project_next, send_hidden)
    inverse_rms = lax.rsqrt(summed[:, QW : QW + 1] / D + 1e-05)
    result = (summed[:, :QW] * inverse_rms).astype(jnp.bfloat16)
    return (section_shift(result[None], 1), in_hbm(stream))


def solution(mesh):
    return jax.shard_map(
        body,
        mesh=mesh,
        in_specs=(
            P("section", ("outer", "inner"), None),
            P(),
            P("section", None, ("outer", "inner")),
            P("section", None, ("outer", "inner")),
            P("section", ("outer", "inner")),
            P("section", ("outer", "inner"), None),
        ),
        out_specs=(P("section", ("outer", "inner"), None), P("section", None, ("outer", "inner"))),
        check_vma=False,
    )
```

```python
import functools

import jax
import jax.numpy as jnp
from jax import lax
from jax.experimental import pallas as pl
from jax.experimental.pallas import tpu as pltpu
from jax.sharding import PartitionSpec as P

D = 16384
HQ = 8
HD = 128
QW = 1280
SUB = 64
PW = QW + 128
NX = 4
NZ = 8
SHARD_AXES = ("outer", "inner")
QUAD = (0, -1, 4, 1)
REST = (-2, 3, -3, 2)
X_ORDER = (0, -1, 1, 2)
KEY_BLOCK = 256
SHARES = (80, 48)
VMEM_GRANT = 12 * 1024 * 1024


def shard_of(x, z):
    x = x & (NX - 1)
    z = z & (NZ - 1)
    return (z & 1) * 16 + x * 4 + (z >> 1)


def run_of(here, half, dx, dz):
    return shard_of(here[0] + dx, here[1] + dz) * 2 + half


def shift(value, dx, dz):
    pairs = [
        (shard_of(x, z), shard_of(x + dx, z + dz)) for x in range(NX) for z in range(NZ)
    ]
    return lax.ppermute(value, SHARD_AXES, pairs)


def section_shift(value, by):
    return lax.ppermute(value, "section", [(i, (i + by) % 8) for i in range(8)])


def attend_kernel(sizes, runs, is_first, is_last, here, run_starts, *refs):
    count = len(sizes)
    rows = refs[0]
    chunks = refs[1 : count + 1]
    refs = refs[count + 1 :]
    tokens = rows.shape[0]
    columns = HQ * tokens
    if is_first:
        largest = jnp.full((1, columns), -1e30, jnp.float32)
        total = jnp.zeros((1, columns), jnp.float32)
        acc = jnp.zeros((HD, columns), jnp.float32)
    else:
        largest, total, acc = refs[0][...], refs[1][...], refs[2][...]
        refs = refs[3:]
    stacked = jnp.concatenate([rows[:, h * HD : (h + 1) * HD] for h in range(HQ)], axis=0)
    lane = lax.broadcasted_iota(jnp.int32, (1, tokens), 1)
    query_positions = lane
    for run in range(tokens // SUB):
        start = run_starts[run_of(here, run, 0, 0)] - run * SUB
        query_positions = jnp.where(lane // SUB == run, lane + start, query_positions)
    row_index = lax.broadcasted_iota(jnp.int32, (SUB, tokens), 0)
    factor = HD ** (-0.5) * 1.4426950408889634
    run = 0
    for chunk, size in zip(chunks, sizes):
        for start in range(0, size, KEY_BLOCK):
            keys = chunk[pl.ds(start, KEY_BLOCK), :HD]
            values = chunk[pl.ds(start, KEY_BLOCK), HD:]
            scores = lax.dot_general(
                keys, stacked, (((1,), (1,)), ((), ())), preferred_element_type=jnp.float32
            )
            masked = []
            for part in range(KEY_BLOCK // SUB):
                start_here = run_starts[run_of(here, *runs[run])]
                visible = row_index + start_here <= query_positions
                visible = jnp.concatenate([visible] * HQ, axis=1)
                block = scores[part * SUB : (part + 1) * SUB] * factor
                masked.append(jnp.where(visible, block, -jnp.inf))
                run += 1
            masked = jnp.concatenate(masked, axis=0)
            new_largest = jnp.maximum(largest, jnp.max(masked, axis=0, keepdims=True))
            weights = jnp.exp2(masked - new_largest)
            keep = jnp.exp2(largest - new_largest)
            total = total * keep + jnp.sum(weights, axis=0, keepdims=True)
            acc = acc * keep + lax.dot_general(
                values,
                weights.astype(jnp.bfloat16),
                (((0,), (0,)), ((), ())),
                preferred_element_type=jnp.float32,
            )
            largest = new_largest
    if is_last:
        mixed = acc / total
        for h in range(HQ):
            turned = jnp.transpose(mixed[:, h * tokens : (h + 1) * tokens]).astype(jnp.bfloat16)
            refs[0][:, h * HD : (h + 1) * HD] = turned[: SHARES[0]]
            refs[1][:, h * HD : (h + 1) * HD] = turned[SHARES[0] :]
    else:
        refs[0][...], refs[1][...], refs[2][...] = largest, total, acc


def attend(here, run_starts, rows, chunks, runs, state, is_last=False):
    sizes = [chunk.shape[0] for chunk in chunks]
    columns = HQ * rows.shape[0]
    smem = pl.BlockSpec(memory_space=pltpu.SMEM)
    vmem = pl.BlockSpec(memory_space=pltpu.VMEM)
    if is_last:
        out_shape = [jax.ShapeDtypeStruct((share, HQ * HD), jnp.bfloat16) for share in SHARES]
    else:
        out_shape = [
            jax.ShapeDtypeStruct((1, columns), jnp.float32),
            jax.ShapeDtypeStruct((1, columns), jnp.float32),
            jax.ShapeDtypeStruct((HD, columns), jnp.float32),
        ]
    return pl.pallas_call(
        functools.partial(attend_kernel, sizes, runs, not state, is_last),
        out_shape=out_shape,
        in_specs=[smem, smem] + [vmem] * (1 + len(chunks) + len(state)),
        out_specs=[vmem] * len(out_shape),
        compiler_params=pltpu.CompilerParams(vmem_limit_bytes=16 * 1024 * 1024),
        cost_estimate=pl.CostEstimate(
            flops=8 * sum(sizes) * columns * HD,
            bytes_accessed=4 * columns * HD,
            transcendentals=sum(sizes) * columns,
        ),
    )(here, run_starts, rows, *chunks, *state)


def nearest(value):
    return value, shift(value, 0, 1), shift(value, 0, 4), shift(value, 0, -1)


def farther(quad):
    rows = quad.shape[0] // 4
    return shift(quad[rows : 3 * rows], 0, 1), shift(quad[2 * rows :], 0, -1)


def attention(here, run_starts, rows, send_weight):
    quad = jnp.concatenate(nearest(rows[:, HQ * HD :]), axis=0)
    step = functools.partial(attend, here, run_starts, rows)

    def column(dx, order):
        return [(part, dx, dz) for dz in order for part in range(2)]

    quad, weight_next = send_weight(quad)
    rest = farther(quad)
    left_quad, right_quad = shift(quad, 1, 0), shift(quad, -1, 0)
    state = step([quad], column(0, QUAD), [])
    rest, state = lax.optimization_barrier((jnp.concatenate(rest, axis=0), state))
    left_rest, right_rest = shift(rest, 1, 0), shift(rest, -1, 0)
    far_quad = shift(left_quad, 1, 0)
    state = step(
        [left_quad, right_quad, rest], column(-1, QUAD) + column(1, QUAD) + column(0, REST), state
    )
    right_rest, state = lax.optimization_barrier((right_rest, state))
    far_rest = shift(right_rest, -1, 0)
    runs = column(-1, REST) + column(1, REST) + column(2, QUAD)
    state = step([left_rest, right_rest, far_quad], runs, state)
    state, weight_next = lax.optimization_barrier((state, weight_next))
    return step([far_rest], column(2, REST), state, True), weight_next


def add(*terms):
    total = terms[0].astype(jnp.float32)
    for term in terms[1:]:
        total = total + term.astype(jnp.float32)
    return total.astype(jnp.bfloat16)


def project_kernel(pieces, kept, here, *refs):
    weight_out, residual, weight_next = refs[:3]
    chunks = refs[3 : 3 + len({piece[0] for piece in pieces})]
    outs = refs[3 + len(chunks) + kept :]
    hidden, parts = outs[0], outs[1:]
    for chunk, start, runs, part, part_start in pieces:
        share = SHARES[runs[0][0]]
        size = len(runs) * share
        product = jnp.dot(
            chunks[chunk][pl.ds(start, size)], weight_out[...], preferred_element_type=jnp.float32
        )
        rows = []
        for sub, run in enumerate(runs):
            shard = shard_of(here[0] + run[1], here[1] + run[2])
            offset = pl.multiple_of(shard * sum(SHARES) + run[0] * SHARES[0], 16)
            sums = residual[pl.ds(offset, share)].astype(jnp.float32)
            sums = (sums + product[sub * share : (sub + 1) * share]).astype(jnp.bfloat16)
            hidden[pl.ds(offset, share)] = sums
            rows.append(sums)
        rows = jnp.concatenate(rows, axis=0)
        place = pl.ds(part_start, size)
        parts[part][place, :QW] = jnp.dot(
            rows, weight_next[...], preferred_element_type=jnp.float32
        ).astype(jnp.bfloat16)
        wide = rows.astype(jnp.float32)
        squares = jnp.sum(wide * wide, axis=1, keepdims=True)
        parts[part][place, QW:] = jnp.broadcast_to(squares, (size, PW - QW)).astype(jnp.bfloat16)


def project(here, weights, residual, hidden, chunks, pieces, part_rows, started=()):
    total = sum(chunk.shape[0] for chunk in chunks)
    width = residual.shape[1]
    kept = [*hidden, *started]
    vmem = pl.BlockSpec(memory_space=pltpu.VMEM)
    hidden, *parts = pl.pallas_call(
        functools.partial(project_kernel, pieces, len(kept)),
        out_shape=[jax.ShapeDtypeStruct(residual.shape, residual.dtype)]
        + [jax.ShapeDtypeStruct((rows, PW), jnp.bfloat16) for rows in part_rows],
        in_specs=[pl.BlockSpec(memory_space=pltpu.SMEM)]
        + [vmem] * (3 + len(chunks) + len(kept)),
        out_specs=[vmem] * (1 + len(part_rows)),
        input_output_aliases={4 + len(chunks) + i: i for i in range(len(kept))},
        compiler_params=pltpu.CompilerParams(vmem_limit_bytes=VMEM_GRANT),
        cost_estimate=pl.CostEstimate(
            flops=2 * total * width * (HQ * HD + QW),
            bytes_accessed=2 * total * (HQ * HD + 2 * width + PW) + 2 * width * (HQ * HD + QW),
            transcendentals=0,
        ),
    )(here, weights[0], residual, weights[1], *chunks, *kept)
    return [hidden], parts


def copy_kernel(source, target):
    target[...] = source[...]


def in_hbm(value):
    block = pl.BlockSpec((1, 512, value.shape[2]), lambda i: (0, i, 0))
    return pl.pallas_call(
        copy_kernel,
        grid=(value.shape[1] // 512,),
        out_shape=jax.ShapeDtypeStruct(value.shape, value.dtype),
        in_specs=[block],
        out_specs=block,
        cost_estimate=pl.CostEstimate(
            flops=0, bytes_accessed=4 * value.size, transcendentals=0
        ),
    )(value)


class Order:
    def __init__(self):
        self.last = None

    def tie(self, *values):
        if self.last is not None:
            *values, self.last = lax.optimization_barrier((*values, self.last))
        return values if len(values) > 1 else values[0]

    def done(self, *values):
        known = () if self.last is None else (self.last,)
        values = lax.optimization_barrier((*values, *known))[: len(values)]
        self.last = values[-1]
        return values if len(values) > 1 else values[0]


def exchange(first, second, project_next, send_hidden):
    pair_rows, quad_rows, line_rows = 2 * SHARES[0], 4 * SHARES[0], NX * SHARES[1]

    def column(dx, order):
        return [(0, dx, dz) for dz in order]

    def line(order, dz):
        return [(1, dx, dz) for dx in order]

    quad = nearest(first)
    row = second, shift(second, 1, 0), shift(second, -1, 0), shift(second, 2, 0)
    quad, row = lax.optimization_barrier((quad, row))
    quad, row = lax.optimization_barrier((jnp.concatenate(quad, axis=0), row))
    row = jnp.concatenate(row, axis=0)
    up_rest, down_rest = farther(quad)
    up1, down1 = shift(row, 0, 1), shift(row, 0, -1)
    left_quad, right_quad = shift(quad, 1, 0), shift(quad, -1, 0)
    (p_row, p_head), (up_rest, down_rest) = project_next(
        [row, quad],
        [(0, 0, line(X_ORDER, 0), 0, 0), (1, 0, column(0, QUAD), 1, 0)],
        [line_rows, quad_rows],
        [],
        [up_rest, down_rest],
    )
    rest = jnp.concatenate([up_rest, down_rest], axis=0)
    left_rest, right_rest = shift(rest, 1, 0), shift(rest, -1, 0)
    up2, down2 = shift(up1, 0, 1), shift(down1, 0, -1)
    (p_up1, p_down1), (left_quad, right_quad) = project_next(
        [up1, down1],
        [(0, 0, line(X_ORDER, -1), 0, 0), (1, 0, line(X_ORDER, 1), 1, 0)],
        [line_rows] * 2,
        [],
        [left_quad, right_quad],
    )
    far_quad = shift(left_quad, 1, 0)
    (to_right_head, to_left_head, p_right_head, p_left_head, p_tail), (up2, down2) = project_next(
        [left_quad, right_quad, rest],
        [
            (0, 0, column(-1, QUAD[:2]), 1, pair_rows),
            (0, pair_rows, column(-1, QUAD[2:]), 3, 0),
            (1, 0, column(1, QUAD[:2]), 2, 0),
            (1, pair_rows, column(1, QUAD[2:]), 0, pair_rows),
            (2, 0, column(0, REST), 4, 0),
        ],
        [quad_rows, quad_rows, pair_rows, pair_rows, quad_rows],
        [],
        [up2, down2],
    )
    up3, down3 = shift(up2, 0, 1), shift(down2, 0, -1)
    (p_up2, p_down2), (left_rest, right_rest) = project_next(
        [up2, down2],
        [(0, 0, line(X_ORDER, -2), 0, 0), (1, 0, line(X_ORDER, 2), 1, 0)],
        [line_rows] * 2,
        [],
        [left_rest, right_rest],
    )
    far_rest = shift(right_rest, -1, 0)
    parts, (up3, down3) = project_next(
        [far_quad, left_rest, right_rest],
        [
            (0, 0, column(2, QUAD[:2]), 0, 0),
            (0, pair_rows, column(2, QUAD[2:]), 1, 0),
            (1, 0, column(-1, REST[:2]), 3, pair_rows),
            (1, pair_rows, column(-1, REST[2:]), 5, 0),
            (2, 0, column(1, REST[:2]), 4, 0),
            (2, pair_rows, column(1, REST[2:]), 2, pair_rows),
        ],
        [quad_rows] * 4 + [pair_rows] * 2,
        [to_right_head, to_left_head],
        [up3, down3],
    )
    to_right_head, to_left_head, to_right_tail, to_left_tail, p_right_tail, p_left_tail = parts
    left_head, right_head = shift(to_right_head, 1, 0), shift(to_left_head, -1, 0)
    up4, down4 = shift(up3[: line_rows // 2], 0, 1), shift(down3[line_rows // 2 :], 0, -1)
    (to_right_tail, to_left_tail, p_up3, p_down3), (up4, down4) = project_next(
        [far_rest, up3, down3],
        [
            (0, 0, column(2, REST[:2]), 0, 0),
            (0, pair_rows, column(2, REST[2:]), 1, 0),
            (1, 0, line(X_ORDER, -3), 2, 0),
            (2, 0, line(X_ORDER, 3), 3, 0),
        ],
        [quad_rows, quad_rows, line_rows, line_rows],
        [to_right_tail, to_left_tail],
        [up4, down4],
    )
    left_tail, right_tail = shift(to_right_tail, 1, 0), shift(to_left_tail, -1, 0)
    (p_up4, p_down4), _ = project_next(
        [up4, down4],
        [(0, 0, line(X_ORDER[:2], 4), 0, 0), (1, 0, line(X_ORDER[2:], 4), 1, 0)],
        [line_rows // 2] * 2,
        [],
        [],
    )
    top, bottom = shift(p_up4, 0, -1), shift(p_down4, 0, 1)

    order = Order()
    cut = line_rows // 2
    left_head, right_head = order.done(left_head, right_head)
    p_up3, p_down3 = order.tie(p_up3, p_down3)
    p_up3 = jnp.concatenate([add(p_up3[:cut], top), p_up3[cut:]], axis=0)
    p_down3 = jnp.concatenate([p_down3[:cut], add(p_down3[cut:], bottom)], axis=0)
    p_up3, p_down3 = order.done(p_up3, p_down3)
    top, bottom = shift(p_up3, 0, -1), shift(p_down3, 0, 1)
    stream = send_hidden(order)
    p_up2, p_down2 = order.tie(p_up2, p_down2)
    p_up2, p_down2 = order.done(add(p_up2, top), add(p_down2, bottom))
    top, bottom = shift(p_up2, 0, -1), shift(p_down2, 0, 1)
    p_right_tail, p_left_tail = order.tie(p_right_tail, p_left_tail)
    p_right_tail, p_left_tail = order.done(
        add(p_right_tail, left_tail[:pair_rows]), add(p_left_tail, right_tail[:pair_rows])
    )
    passed_right, passed_left = shift(p_right_tail, 1, 0), shift(p_left_tail, -1, 0)
    p_up1, p_down1 = order.tie(p_up1, p_down1)
    p_up1, p_down1 = order.done(add(p_up1, top), add(p_down1, bottom))
    top, bottom = shift(p_up1, 0, -1), shift(p_down1, 0, 1)
    p_tail = order.tie(p_tail)
    upper, lower = order.done(
        add(p_tail[:pair_rows], right_tail[pair_rows:], passed_right),
        add(p_tail[pair_rows:], left_tail[pair_rows:], passed_left),
    )
    from_above, from_below = shift(upper, 0, -1), shift(lower, 0, 1)
    p_right_head, p_left_head = order.tie(p_right_head, p_left_head)
    p_right_head, p_left_head = order.done(
        add(p_right_head, left_head[:pair_rows]), add(p_left_head, right_head[:pair_rows])
    )
    passed_right, passed_left = shift(p_right_head, 1, 0), shift(p_left_head, -1, 0)
    p_row, stream = order.tie(p_row, stream)
    row = order.done(add(p_row, top, bottom))
    share = SHARES[1]
    terms = [
        row[:share],
        shift(row[share : 2 * share], -1, 0),
        shift(row[2 * share : 3 * share], 1, 0),
        shift(row[3 * share :], 2, 0),
    ]
    p_head, from_above, from_below = order.tie(p_head, from_above, from_below)
    p_head = order.done(
        jnp.concatenate(
            [
                add(p_head[:pair_rows], right_head[pair_rows:], passed_right),
                add(p_head[pair_rows:], left_head[pair_rows:], passed_left),
            ],
            axis=0,
        )
    )
    share = SHARES[0]
    behind = add(p_head[share : 2 * share], from_above[:share])
    opposite = add(p_head[2 * share : 3 * share], from_above[share:], from_below[:share])
    ahead = add(p_head[3 * share :], from_below[share:])
    others = [shift(opposite, 0, 4), p_head[:share], shift(behind, 0, -1), shift(ahead, 0, 1)]
    first = sum(term.astype(jnp.float32) for term in others)
    second = sum(term.astype(jnp.float32) for term in terms)
    return jnp.concatenate([first, second], axis=0), stream


def body(projected, positions, out_weight, residual, norm_gain, next_weight):
    local_rows = projected[0]
    outer = lax.axis_index("outer")
    inner = lax.axis_index("inner")
    here = jnp.stack([outer % NX, inner * 2 + outer // NX])

    def send_weight(quad):
        quad, weight = lax.optimization_barrier((quad, next_weight[0]))
        scaled = weight.astype(jnp.float32) * norm_gain[0].astype(jnp.float32)[:, None]
        return quad, section_shift(scaled.astype(jnp.bfloat16), -1)

    (first, second), weight_next = attention(
        here, positions[::SUB], local_rows, send_weight
    )
    hidden = []

    def project_next(chunks, pieces, part_rows, started, held):
        outs, parts = project(
            here,
            (out_weight[0], weight_next),
            residual[0],
            hidden,
            chunks,
            pieces,
            part_rows,
            started,
        )
        if held:
            outs[0], held = lax.optimization_barrier((outs[0], held))
        hidden[:] = outs
        return parts, held

    def send_hidden(order):
        return section_shift(order.tie(hidden[0])[None], 1)

    summed, stream = exchange(first, second, project_next, send_hidden)
    inverse_rms = lax.rsqrt(summed[:, QW : QW + 1] / D + 1e-05)
    result = (summed[:, :QW] * inverse_rms).astype(jnp.bfloat16)
    return (section_shift(result[None], 1), in_hbm(stream))


def solution(mesh):
    return jax.shard_map(
        body,
        mesh=mesh,
        in_specs=(
            P("section", ("outer", "inner"), None),
            P(),
            P("section", None, ("outer", "inner")),
            P("section", None, ("outer", "inner")),
            P("section", ("outer", "inner")),
            P("section", ("outer", "inner"), None),
        ),
        out_specs=(P("section", ("outer", "inner"), None), P("section", None, ("outer", "inner"))),
        check_vma=False,
    )
```

```python
import functools

import jax
import jax.numpy as jnp
from jax import lax
from jax.experimental import pallas as pl
from jax.experimental.pallas import tpu as pltpu
from jax.sharding import PartitionSpec as P

D = 16384
HQ = 8
HD = 128
QW = 1280
SUB = 64
PW = QW + 128
NX = 4
NZ = 8
SHARD_AXES = ("outer", "inner")
QUAD = (0, -1, 4, 1)
REST = (-2, 3, -3, 2)
X_ORDER = (0, -1, 1, 2)
KEY_BLOCK = 256
SHARES = (80, 48)
VMEM_GRANT = 12 * 1024 * 1024


def shard_of(x, z):
    x = x & (NX - 1)
    z = z & (NZ - 1)
    return (z & 1) * 16 + x * 4 + (z >> 1)


def run_of(here, half, dx, dz):
    return shard_of(here[0] + dx, here[1] + dz) * 2 + half


def shift(value, dx, dz):
    pairs = [
        (shard_of(x, z), shard_of(x + dx, z + dz)) for x in range(NX) for z in range(NZ)
    ]
    return lax.ppermute(value, SHARD_AXES, pairs)


def section_shift(value, by):
    return lax.ppermute(value, "section", [(i, (i + by) % 8) for i in range(8)])


def attend_kernel(sizes, runs, is_first, is_last, here, run_starts, *refs):
    count = len(sizes)
    rows = refs[0]
    chunks = refs[1 : count + 1]
    refs = refs[count + 1 :]
    tokens = rows.shape[0]
    columns = HQ * tokens
    if is_first:
        largest = jnp.full((1, columns), -1e30, jnp.float32)
        total = jnp.zeros((1, columns), jnp.float32)
        acc = jnp.zeros((HD, columns), jnp.float32)
    else:
        largest, total, acc = refs[0][...], refs[1][...], refs[2][...]
        refs = refs[3:]
    stacked = jnp.concatenate([rows[:, h * HD : (h + 1) * HD] for h in range(HQ)], axis=0)
    lane = lax.broadcasted_iota(jnp.int32, (1, tokens), 1)
    query_positions = lane
    for run in range(tokens // SUB):
        start = run_starts[run_of(here, run, 0, 0)] - run * SUB
        query_positions = jnp.where(lane // SUB == run, lane + start, query_positions)
    row_index = lax.broadcasted_iota(jnp.int32, (SUB, tokens), 0)
    factor = HD ** (-0.5) * 1.4426950408889634
    run = 0
    for chunk, size in zip(chunks, sizes):
        for start in range(0, size, KEY_BLOCK):
            keys = chunk[pl.ds(start, KEY_BLOCK), :HD]
            values = chunk[pl.ds(start, KEY_BLOCK), HD:]
            scores = lax.dot_general(
                keys, stacked, (((1,), (1,)), ((), ())), preferred_element_type=jnp.float32
            )
            masked = []
            for part in range(KEY_BLOCK // SUB):
                start_here = run_starts[run_of(here, *runs[run])]
                visible = row_index + start_here <= query_positions
                visible = jnp.concatenate([visible] * HQ, axis=1)
                block = scores[part * SUB : (part + 1) * SUB] * factor
                masked.append(jnp.where(visible, block, -jnp.inf))
                run += 1
            masked = jnp.concatenate(masked, axis=0)
            new_largest = jnp.maximum(largest, jnp.max(masked, axis=0, keepdims=True))
            weights = jnp.exp2(masked - new_largest)
            keep = jnp.exp2(largest - new_largest)
            total = total * keep + jnp.sum(weights, axis=0, keepdims=True)
            acc = acc * keep + lax.dot_general(
                values,
                weights.astype(jnp.bfloat16),
                (((0,), (0,)), ((), ())),
                preferred_element_type=jnp.float32,
            )
            largest = new_largest
    if is_last:
        mixed = acc / total
        for h in range(HQ):
            turned = jnp.transpose(mixed[:, h * tokens : (h + 1) * tokens]).astype(jnp.bfloat16)
            refs[0][:, h * HD : (h + 1) * HD] = turned[: SHARES[0]]
            refs[1][:, h * HD : (h + 1) * HD] = turned[SHARES[0] :]
    else:
        refs[0][...], refs[1][...], refs[2][...] = largest, total, acc


def attend(here, run_starts, rows, chunks, runs, state, is_last=False):
    sizes = [chunk.shape[0] for chunk in chunks]
    columns = HQ * rows.shape[0]
    smem = pl.BlockSpec(memory_space=pltpu.SMEM)
    vmem = pl.BlockSpec(memory_space=pltpu.VMEM)
    if is_last:
        out_shape = [jax.ShapeDtypeStruct((share, HQ * HD), jnp.bfloat16) for share in SHARES]
    else:
        out_shape = [
            jax.ShapeDtypeStruct((1, columns), jnp.float32),
            jax.ShapeDtypeStruct((1, columns), jnp.float32),
            jax.ShapeDtypeStruct((HD, columns), jnp.float32),
        ]
    return pl.pallas_call(
        functools.partial(attend_kernel, sizes, runs, not state, is_last),
        out_shape=out_shape,
        in_specs=[smem, smem] + [vmem] * (1 + len(chunks) + len(state)),
        out_specs=[vmem] * len(out_shape),
        compiler_params=pltpu.CompilerParams(vmem_limit_bytes=16 * 1024 * 1024),
        cost_estimate=pl.CostEstimate(
            flops=8 * sum(sizes) * columns * HD,
            bytes_accessed=4 * columns * HD,
            transcendentals=sum(sizes) * columns,
        ),
    )(here, run_starts, rows, *chunks, *state)


def nearest(value):
    return value, shift(value, 0, 1), shift(value, 0, 4), shift(value, 0, -1)


def farther(quad):
    rows = quad.shape[0] // 4
    return shift(quad[rows : 3 * rows], 0, 1), shift(quad[2 * rows :], 0, -1)


def attention(here, run_starts, rows, send_weight):
    quad = jnp.concatenate(nearest(rows[:, HQ * HD :]), axis=0)
    step = functools.partial(attend, here, run_starts, rows)

    def column(dx, order):
        return [(part, dx, dz) for dz in order for part in range(2)]

    quad, weight_next = send_weight(quad)
    rest = farther(quad)
    left_quad, right_quad = shift(quad, 1, 0), shift(quad, -1, 0)
    state = step([quad], column(0, QUAD), [])
    rest, state = lax.optimization_barrier((jnp.concatenate(rest, axis=0), state))
    left_rest, right_rest = shift(rest, 1, 0), shift(rest, -1, 0)
    far_quad = shift(left_quad, 1, 0)
    state = step(
        [left_quad, right_quad, rest], column(-1, QUAD) + column(1, QUAD) + column(0, REST), state
    )
    right_rest, state = lax.optimization_barrier((right_rest, state))
    far_rest = shift(right_rest, -1, 0)
    runs = column(-1, REST) + column(1, REST) + column(2, QUAD)
    state = step([left_rest, right_rest, far_quad], runs, state)
    state, weight_next = lax.optimization_barrier((state, weight_next))
    return step([far_rest], column(2, REST), state, True), weight_next


def add(*terms):
    total = terms[0].astype(jnp.float32)
    for term in terms[1:]:
        total = total + term.astype(jnp.float32)
    return total.astype(jnp.bfloat16)


def project_kernel(pieces, kept, here, *refs):
    weight_out, residual, weight_next = refs[:3]
    chunks = refs[3 : 3 + len({piece[0] for piece in pieces})]
    outs = refs[3 + len(chunks) + kept :]
    hidden, parts = outs[0], outs[1:]
    for chunk, start, runs, part, part_start in pieces:
        share = SHARES[runs[0][0]]
        size = len(runs) * share
        product = jnp.dot(
            chunks[chunk][pl.ds(start, size)], weight_out[...], preferred_element_type=jnp.float32
        )
        rows = []
        for sub, run in enumerate(runs):
            shard = shard_of(here[0] + run[1], here[1] + run[2])
            offset = pl.multiple_of(shard * sum(SHARES) + run[0] * SHARES[0], 16)
            sums = residual[pl.ds(offset, share)].astype(jnp.float32)
            sums = (sums + product[sub * share : (sub + 1) * share]).astype(jnp.bfloat16)
            hidden[pl.ds(offset, share)] = sums
            rows.append(sums)
        rows = jnp.concatenate(rows, axis=0)
        place = pl.ds(part_start, size)
        parts[part][place, :QW] = jnp.dot(
            rows, weight_next[...], preferred_element_type=jnp.float32
        ).astype(jnp.bfloat16)
        wide = rows.astype(jnp.float32)
        squares = jnp.sum(wide * wide, axis=1, keepdims=True)
        parts[part][place, QW:] = jnp.broadcast_to(squares, (size, PW - QW)).astype(jnp.bfloat16)


def project(here, weights, residual, hidden, chunks, pieces, part_rows, started=()):
    total = sum(chunk.shape[0] for chunk in chunks)
    width = residual.shape[1]
    kept = [*hidden, *started]
    vmem = pl.BlockSpec(memory_space=pltpu.VMEM)
    hidden, *parts = pl.pallas_call(
        functools.partial(project_kernel, pieces, len(kept)),
        out_shape=[jax.ShapeDtypeStruct(residual.shape, residual.dtype)]
        + [jax.ShapeDtypeStruct((rows, PW), jnp.bfloat16) for rows in part_rows],
        in_specs=[pl.BlockSpec(memory_space=pltpu.SMEM)]
        + [vmem] * (3 + len(chunks) + len(kept)),
        out_specs=[vmem] * (1 + len(part_rows)),
        input_output_aliases={4 + len(chunks) + i: i for i in range(len(kept))},
        compiler_params=pltpu.CompilerParams(vmem_limit_bytes=VMEM_GRANT),
        cost_estimate=pl.CostEstimate(
            flops=2 * total * width * (HQ * HD + QW),
            bytes_accessed=2 * total * (HQ * HD + 2 * width + PW) + 2 * width * (HQ * HD + QW),
            transcendentals=0,
        ),
    )(here, weights[0], residual, weights[1], *chunks, *kept)
    return [hidden], parts


def copy_kernel(source, target):
    target[...] = source[...]


def in_hbm(value):
    block = pl.BlockSpec((1, 512, value.shape[2]), lambda i: (0, i, 0))
    return pl.pallas_call(
        copy_kernel,
        grid=(value.shape[1] // 512,),
        out_shape=jax.ShapeDtypeStruct(value.shape, value.dtype),
        in_specs=[block],
        out_specs=block,
        cost_estimate=pl.CostEstimate(
            flops=0, bytes_accessed=4 * value.size, transcendentals=0
        ),
    )(value)


class Order:
    def __init__(self):
        self.last = None

    def tie(self, *values):
        if self.last is not None:
            *values, self.last = lax.optimization_barrier((*values, self.last))
        return values if len(values) > 1 else values[0]

    def done(self, *values):
        known = () if self.last is None else (self.last,)
        values = lax.optimization_barrier((*values, *known))[: len(values)]
        self.last = values[-1]
        return values if len(values) > 1 else values[0]


def exchange(first, second, project_next, send_hidden):
    pair_rows, quad_rows, line_rows = 2 * SHARES[0], 4 * SHARES[0], NX * SHARES[1]

    def column(dx, order):
        return [(0, dx, dz) for dz in order]

    def line(order, dz):
        return [(1, dx, dz) for dx in order]

    quad = nearest(first)
    row = second, shift(second, 1, 0), shift(second, -1, 0), shift(second, 2, 0)
    quad, row = lax.optimization_barrier((quad, row))
    quad, row = lax.optimization_barrier((jnp.concatenate(quad, axis=0), row))
    row = jnp.concatenate(row, axis=0)
    up_rest, down_rest = farther(quad)
    up1, down1 = shift(row, 0, 1), shift(row, 0, -1)
    left_quad, right_quad = shift(quad, 1, 0), shift(quad, -1, 0)
    (p_row, p_head), (up_rest, down_rest) = project_next(
        [row, quad],
        [(0, 0, line(X_ORDER, 0), 0, 0), (1, 0, column(0, QUAD), 1, 0)],
        [line_rows, quad_rows],
        [],
        [up_rest, down_rest],
    )
    rest = jnp.concatenate([up_rest, down_rest], axis=0)
    left_rest, right_rest = shift(rest, 1, 0), shift(rest, -1, 0)
    up2, down2 = shift(up1, 0, 1), shift(down1, 0, -1)
    (p_up1, p_down1), (left_quad, right_quad) = project_next(
        [up1, down1],
        [(0, 0, line(X_ORDER, -1), 0, 0), (1, 0, line(X_ORDER, 1), 1, 0)],
        [line_rows] * 2,
        [],
        [left_quad, right_quad],
    )
    far_quad = shift(left_quad, 1, 0)
    (to_right_head, to_left_head, p_right_head, p_left_head, p_tail), (up2, down2) = project_next(
        [left_quad, right_quad, rest],
        [
            (0, 0, column(-1, QUAD[:2]), 1, pair_rows),
            (0, pair_rows, column(-1, QUAD[2:]), 3, 0),
            (1, 0, column(1, QUAD[:2]), 2, 0),
            (1, pair_rows, column(1, QUAD[2:]), 0, pair_rows),
            (2, 0, column(0, REST), 4, 0),
        ],
        [quad_rows, quad_rows, pair_rows, pair_rows, quad_rows],
        [],
        [up2, down2],
    )
    up3, down3 = shift(up2, 0, 1), shift(down2, 0, -1)
    (p_up2, p_down2), (left_rest, right_rest) = project_next(
        [up2, down2],
        [(0, 0, line(X_ORDER, -2), 0, 0), (1, 0, line(X_ORDER, 2), 1, 0)],
        [line_rows] * 2,
        [],
        [left_rest, right_rest],
    )
    far_rest = shift(right_rest, -1, 0)
    parts, (up3, down3) = project_next(
        [far_quad, left_rest, right_rest],
        [
            (0, 0, column(2, QUAD[:2]), 0, 0),
            (0, pair_rows, column(2, QUAD[2:]), 1, 0),
            (1, 0, column(-1, REST[:2]), 3, pair_rows),
            (1, pair_rows, column(-1, REST[2:]), 5, 0),
            (2, 0, column(1, REST[:2]), 4, 0),
            (2, pair_rows, column(1, REST[2:]), 2, pair_rows),
        ],
        [quad_rows] * 4 + [pair_rows] * 2,
        [to_right_head, to_left_head],
        [up3, down3],
    )
    to_right_head, to_left_head, to_right_tail, to_left_tail, p_right_tail, p_left_tail = parts
    left_head, right_head = shift(to_right_head, 1, 0), shift(to_left_head, -1, 0)
    up4, down4 = shift(up3[: line_rows // 2], 0, 1), shift(down3[line_rows // 2 :], 0, -1)
    (to_right_tail, to_left_tail, p_up3, p_down3), (up4, down4) = project_next(
        [far_rest, up3, down3],
        [
            (0, 0, column(2, REST[:2]), 0, 0),
            (0, pair_rows, column(2, REST[2:]), 1, 0),
            (1, 0, line(X_ORDER, -3), 2, 0),
            (2, 0, line(X_ORDER, 3), 3, 0),
        ],
        [quad_rows, quad_rows, line_rows, line_rows],
        [to_right_tail, to_left_tail],
        [up4, down4],
    )
    left_tail, right_tail = shift(to_right_tail, 1, 0), shift(to_left_tail, -1, 0)
    (p_up4, p_down4), _ = project_next(
        [up4, down4],
        [(0, 0, line(X_ORDER[:2], 4), 0, 0), (1, 0, line(X_ORDER[2:], 4), 1, 0)],
        [line_rows // 2] * 2,
        [],
        [],
    )
    top, bottom = shift(p_up4, 0, -1), shift(p_down4, 0, 1)

    order = Order()
    cut = line_rows // 2
    left_head, right_head = order.done(left_head, right_head)
    p_up3, p_down3 = order.tie(p_up3, p_down3)
    p_up3 = jnp.concatenate([add(p_up3[:cut], top), p_up3[cut:]], axis=0)
    p_down3 = jnp.concatenate([p_down3[:cut], add(p_down3[cut:], bottom)], axis=0)
    p_up3, p_down3 = order.done(p_up3, p_down3)
    top, bottom = shift(p_up3, 0, -1), shift(p_down3, 0, 1)
    stream = send_hidden(order)
    p_up2, p_down2 = order.tie(p_up2, p_down2)
    p_up2, p_down2 = order.done(add(p_up2, top), add(p_down2, bottom))
    top, bottom = shift(p_up2, 0, -1), shift(p_down2, 0, 1)
    p_right_tail, p_left_tail = order.tie(p_right_tail, p_left_tail)
    to_right = [add(p_right_tail, left_tail[:pair_rows]), add(p_right_head, left_head[:pair_rows])]
    to_left = [add(p_left_tail, right_tail[:pair_rows]), add(p_left_head, right_head[:pair_rows])]
    to_right, to_left = order.done(
        jnp.concatenate(to_right, axis=0), jnp.concatenate(to_left, axis=0)
    )
    passed_right, passed_left = shift(to_right, 1, 0), shift(to_left, -1, 0)
    p_up1, p_down1 = order.tie(p_up1, p_down1)
    p_up1, p_down1 = order.done(add(p_up1, top), add(p_down1, bottom))
    top, bottom = shift(p_up1, 0, -1), shift(p_down1, 0, 1)
    p_tail = order.tie(p_tail)
    upper, lower = order.done(
        add(p_tail[:pair_rows], right_tail[pair_rows:], passed_right[:pair_rows]),
        add(p_tail[pair_rows:], left_tail[pair_rows:], passed_left[:pair_rows]),
    )
    from_above, from_below = shift(upper, 0, -1), shift(lower, 0, 1)
    p_row = order.tie(p_row)
    row = order.done(add(p_row, top, bottom))
    share = SHARES[1]
    terms = [
        row[:share],
        shift(row[share : 2 * share], -1, 0),
        shift(row[2 * share : 3 * share], 1, 0),
        shift(row[3 * share :], 2, 0),
    ]
    p_head, stream = order.tie(p_head, stream)
    p_head = order.done(
        jnp.concatenate(
            [
                add(p_head[:pair_rows], right_head[pair_rows:], passed_right[pair_rows:]),
                add(p_head[pair_rows:], left_head[pair_rows:], passed_left[pair_rows:]),
            ],
            axis=0,
        )
    )
    share = SHARES[0]
    behind = add(p_head[share : 2 * share], from_above[:share])
    opposite = add(p_head[2 * share : 3 * share], from_above[share:], from_below[:share])
    ahead = add(p_head[3 * share :], from_below[share:])
    others = [shift(opposite, 0, 4), p_head[:share], shift(behind, 0, -1), shift(ahead, 0, 1)]
    first = sum(term.astype(jnp.float32) for term in others)
    second = sum(term.astype(jnp.float32) for term in terms)
    return jnp.concatenate([first, second], axis=0), stream


def body(projected, positions, out_weight, residual, norm_gain, next_weight):
    local_rows = projected[0]
    outer = lax.axis_index("outer")
    inner = lax.axis_index("inner")
    here = jnp.stack([outer % NX, inner * 2 + outer // NX])

    def send_weight(quad):
        quad, weight = lax.optimization_barrier((quad, next_weight[0]))
        scaled = weight.astype(jnp.float32) * norm_gain[0].astype(jnp.float32)[:, None]
        return quad, section_shift(scaled.astype(jnp.bfloat16), -1)

    (first, second), weight_next = attention(
        here, positions[::SUB], local_rows, send_weight
    )
    hidden = []

    def project_next(chunks, pieces, part_rows, started, held):
        outs, parts = project(
            here,
            (out_weight[0], weight_next),
            residual[0],
            hidden,
            chunks,
            pieces,
            part_rows,
            started,
        )
        if held:
            outs[0], held = lax.optimization_barrier((outs[0], held))
        hidden[:] = outs
        return parts, held

    def send_hidden(order):
        return section_shift(order.tie(hidden[0])[None], 1)

    summed, stream = exchange(first, second, project_next, send_hidden)
    inverse_rms = lax.rsqrt(summed[:, QW : QW + 1] / D + 1e-05)
    result = (summed[:, :QW] * inverse_rms).astype(jnp.bfloat16)
    return (section_shift(result[None], 1), in_hbm(stream))


def solution(mesh):
    return jax.shard_map(
        body,
        mesh=mesh,
        in_specs=(
            P("section", ("outer", "inner"), None),
            P(),
            P("section", None, ("outer", "inner")),
            P("section", None, ("outer", "inner")),
            P("section", ("outer", "inner")),
            P("section", ("outer", "inner"), None),
        ),
        out_specs=(P("section", ("outer", "inner"), None), P("section", None, ("outer", "inner"))),
        check_vma=False,
    )
```

```python
import functools

import jax
import jax.numpy as jnp
from jax import lax
from jax.experimental import pallas as pl
from jax.experimental.pallas import tpu as pltpu
from jax.sharding import PartitionSpec as P

D = 16384
HQ = 8
HD = 128
QW = 1280
SUB = 64
PW = QW + 128
NX = 4
NZ = 8
SHARD_AXES = ("outer", "inner")
QUAD = (0, -1, 4, 1)
REST = (-2, 3, -3, 2)
X_ORDER = (0, -1, 1, 2)
KEY_BLOCK = 256
SHARES = (80, 48)
VMEM_GRANT = 12 * 1024 * 1024


def shard_of(x, z):
    x = x & (NX - 1)
    z = z & (NZ - 1)
    return (z & 1) * 16 + x * 4 + (z >> 1)


def run_of(here, half, dx, dz):
    return shard_of(here[0] + dx, here[1] + dz) * 2 + half


def shift(value, dx, dz):
    pairs = [
        (shard_of(x, z), shard_of(x + dx, z + dz)) for x in range(NX) for z in range(NZ)
    ]
    return lax.ppermute(value, SHARD_AXES, pairs)


def section_shift(value, by):
    return lax.ppermute(value, "section", [(i, (i + by) % 8) for i in range(8)])


def attend_kernel(sizes, runs, is_first, is_last, here, run_starts, *refs):
    count = len(sizes)
    rows = refs[0]
    chunks = refs[1 : count + 1]
    refs = refs[count + 1 :]
    tokens = rows.shape[0]
    columns = HQ * tokens
    if is_first:
        largest = jnp.full((1, columns), -1e30, jnp.float32)
        total = jnp.zeros((1, columns), jnp.float32)
        acc = jnp.zeros((HD, columns), jnp.float32)
    else:
        largest, total, acc = refs[0][...], refs[1][...], refs[2][...]
        refs = refs[3:]
    stacked = jnp.concatenate([rows[:, h * HD : (h + 1) * HD] for h in range(HQ)], axis=0)
    lane = lax.broadcasted_iota(jnp.int32, (1, tokens), 1)
    query_positions = lane
    for run in range(tokens // SUB):
        start = run_starts[run_of(here, run, 0, 0)] - run * SUB
        query_positions = jnp.where(lane // SUB == run, lane + start, query_positions)
    row_index = lax.broadcasted_iota(jnp.int32, (SUB, tokens), 0)
    factor = HD ** (-0.5) * 1.4426950408889634
    run = 0
    for chunk, size in zip(chunks, sizes):
        for start in range(0, size, KEY_BLOCK):
            keys = chunk[pl.ds(start, KEY_BLOCK), :HD]
            values = chunk[pl.ds(start, KEY_BLOCK), HD:]
            scores = lax.dot_general(
                keys, stacked, (((1,), (1,)), ((), ())), preferred_element_type=jnp.float32
            )
            masked = []
            for part in range(KEY_BLOCK // SUB):
                start_here = run_starts[run_of(here, *runs[run])]
                visible = row_index + start_here <= query_positions
                visible = jnp.concatenate([visible] * HQ, axis=1)
                block = scores[part * SUB : (part + 1) * SUB] * factor
                masked.append(jnp.where(visible, block, -jnp.inf))
                run += 1
            masked = jnp.concatenate(masked, axis=0)
            new_largest = jnp.maximum(largest, jnp.max(masked, axis=0, keepdims=True))
            weights = jnp.exp2(masked - new_largest)
            keep = jnp.exp2(largest - new_largest)
            total = total * keep + jnp.sum(weights, axis=0, keepdims=True)
            acc = acc * keep + lax.dot_general(
                values,
                weights.astype(jnp.bfloat16),
                (((0,), (0,)), ((), ())),
                preferred_element_type=jnp.float32,
            )
            largest = new_largest
    if is_last:
        mixed = acc / total
        for h in range(HQ):
            turned = jnp.transpose(mixed[:, h * tokens : (h + 1) * tokens]).astype(jnp.bfloat16)
            refs[0][:, h * HD : (h + 1) * HD] = turned[: SHARES[0]]
            refs[1][:, h * HD : (h + 1) * HD] = turned[SHARES[0] :]
    else:
        refs[0][...], refs[1][...], refs[2][...] = largest, total, acc


def attend(here, run_starts, rows, chunks, runs, state, is_last=False):
    sizes = [chunk.shape[0] for chunk in chunks]
    columns = HQ * rows.shape[0]
    smem = pl.BlockSpec(memory_space=pltpu.SMEM)
    vmem = pl.BlockSpec(memory_space=pltpu.VMEM)
    if is_last:
        out_shape = [jax.ShapeDtypeStruct((share, HQ * HD), jnp.bfloat16) for share in SHARES]
    else:
        out_shape = [
            jax.ShapeDtypeStruct((1, columns), jnp.float32),
            jax.ShapeDtypeStruct((1, columns), jnp.float32),
            jax.ShapeDtypeStruct((HD, columns), jnp.float32),
        ]
    return pl.pallas_call(
        functools.partial(attend_kernel, sizes, runs, not state, is_last),
        out_shape=out_shape,
        in_specs=[smem, smem] + [vmem] * (1 + len(chunks) + len(state)),
        out_specs=[vmem] * len(out_shape),
        compiler_params=pltpu.CompilerParams(vmem_limit_bytes=16 * 1024 * 1024),
        cost_estimate=pl.CostEstimate(
            flops=8 * sum(sizes) * columns * HD,
            bytes_accessed=4 * columns * HD,
            transcendentals=sum(sizes) * columns,
        ),
    )(here, run_starts, rows, *chunks, *state)


def nearest(value):
    return value, shift(value, 0, 1), shift(value, 0, 4), shift(value, 0, -1)


def farther(quad):
    rows = quad.shape[0] // 4
    return shift(quad[rows : 3 * rows], 0, 1), shift(quad[2 * rows :], 0, -1)


def attention(here, run_starts, rows, send_weight):
    quad = jnp.concatenate(nearest(rows[:, HQ * HD :]), axis=0)
    step = functools.partial(attend, here, run_starts, rows)

    def column(dx, order):
        return [(part, dx, dz) for dz in order for part in range(2)]

    quad, weight_next = send_weight(quad)
    rest = farther(quad)
    left_quad, right_quad = shift(quad, 1, 0), shift(quad, -1, 0)
    state = step([quad], column(0, QUAD), [])
    rest, state = lax.optimization_barrier((jnp.concatenate(rest, axis=0), state))
    left_rest, right_rest = shift(rest, 1, 0), shift(rest, -1, 0)
    far_quad = shift(left_quad, 1, 0)
    state = step(
        [left_quad, right_quad, rest], column(-1, QUAD) + column(1, QUAD) + column(0, REST), state
    )
    right_rest, state = lax.optimization_barrier((right_rest, state))
    far_rest = shift(right_rest, -1, 0)
    runs = column(-1, REST) + column(1, REST) + column(2, QUAD)
    state = step([left_rest, right_rest, far_quad], runs, state)
    state, weight_next = lax.optimization_barrier((state, weight_next))
    return step([far_rest], column(2, REST), state, True), weight_next


def add(*terms):
    total = terms[0].astype(jnp.float32)
    for term in terms[1:]:
        total = total + term.astype(jnp.float32)
    return total.astype(jnp.bfloat16)


def project_kernel(pieces, kept, here, *refs):
    weight_out, residual, weight_next = refs[:3]
    chunks = refs[3 : 3 + len({piece[0] for piece in pieces})]
    outs = refs[3 + len(chunks) + kept :]
    hidden, parts = outs[0], outs[1:]
    for chunk, start, runs, part, part_start in pieces:
        share = SHARES[runs[0][0]]
        size = len(runs) * share
        product = jnp.dot(
            chunks[chunk][pl.ds(start, size)], weight_out[...], preferred_element_type=jnp.float32
        )
        rows = []
        for sub, run in enumerate(runs):
            shard = shard_of(here[0] + run[1], here[1] + run[2])
            offset = pl.multiple_of(shard * sum(SHARES) + run[0] * SHARES[0], 16)
            sums = residual[pl.ds(offset, share)].astype(jnp.float32)
            sums = (sums + product[sub * share : (sub + 1) * share]).astype(jnp.bfloat16)
            hidden[pl.ds(offset, share)] = sums
            rows.append(sums)
        rows = jnp.concatenate(rows, axis=0)
        place = pl.ds(part_start, size)
        parts[part][place, :QW] = jnp.dot(
            rows, weight_next[...], preferred_element_type=jnp.float32
        ).astype(jnp.bfloat16)
        wide = rows.astype(jnp.float32)
        squares = jnp.sum(wide * wide, axis=1, keepdims=True)
        parts[part][place, QW:] = jnp.broadcast_to(squares, (size, PW - QW)).astype(jnp.bfloat16)


def project(here, weights, residual, hidden, chunks, pieces, part_rows, started=()):
    total = sum(chunk.shape[0] for chunk in chunks)
    width = residual.shape[1]
    kept = [*hidden, *started]
    vmem = pl.BlockSpec(memory_space=pltpu.VMEM)
    hidden, *parts = pl.pallas_call(
        functools.partial(project_kernel, pieces, len(kept)),
        out_shape=[jax.ShapeDtypeStruct(residual.shape, residual.dtype)]
        + [jax.ShapeDtypeStruct((rows, PW), jnp.bfloat16) for rows in part_rows],
        in_specs=[pl.BlockSpec(memory_space=pltpu.SMEM)]
        + [vmem] * (3 + len(chunks) + len(kept)),
        out_specs=[vmem] * (1 + len(part_rows)),
        input_output_aliases={4 + len(chunks) + i: i for i in range(len(kept))},
        compiler_params=pltpu.CompilerParams(vmem_limit_bytes=VMEM_GRANT),
        cost_estimate=pl.CostEstimate(
            flops=2 * total * width * (HQ * HD + QW),
            bytes_accessed=2 * total * (HQ * HD + 2 * width + PW) + 2 * width * (HQ * HD + QW),
            transcendentals=0,
        ),
    )(here, weights[0], residual, weights[1], *chunks, *kept)
    return [hidden], parts


def copy_kernel(source, target):
    target[...] = source[...]


def in_hbm(value):
    block = pl.BlockSpec((1, 512, value.shape[2]), lambda i: (0, i, 0))
    return pl.pallas_call(
        copy_kernel,
        grid=(value.shape[1] // 512,),
        out_shape=jax.ShapeDtypeStruct(value.shape, value.dtype),
        in_specs=[block],
        out_specs=block,
        cost_estimate=pl.CostEstimate(
            flops=0, bytes_accessed=4 * value.size, transcendentals=0
        ),
    )(value)


class Order:
    def __init__(self):
        self.last = None

    def tie(self, *values):
        if self.last is not None:
            *values, self.last = lax.optimization_barrier((*values, self.last))
        return values if len(values) > 1 else values[0]

    def done(self, *values):
        known = () if self.last is None else (self.last,)
        values = lax.optimization_barrier((*values, *known))[: len(values)]
        self.last = values[-1]
        return values if len(values) > 1 else values[0]


def exchange(first, second, project_next, send_hidden):
    pair_rows, quad_rows, line_rows = 2 * SHARES[0], 4 * SHARES[0], NX * SHARES[1]

    def column(dx, order):
        return [(0, dx, dz) for dz in order]

    def line(order, dz):
        return [(1, dx, dz) for dx in order]

    quad = nearest(first)
    row = second, shift(second, 1, 0), shift(second, -1, 0), shift(second, 2, 0)
    quad, row = lax.optimization_barrier((quad, row))
    quad, row = lax.optimization_barrier((jnp.concatenate(quad, axis=0), row))
    row = jnp.concatenate(row, axis=0)
    up_rest, down_rest = farther(quad)
    up1, down1 = shift(row, 0, 1), shift(row, 0, -1)
    left_quad, right_quad = shift(quad, 1, 0), shift(quad, -1, 0)
    (p_row, p_head), (up_rest, down_rest) = project_next(
        [row, quad],
        [(0, 0, line(X_ORDER, 0), 0, 0), (1, 0, column(0, QUAD), 1, 0)],
        [line_rows, quad_rows],
        [],
        [up_rest, down_rest],
    )
    rest = jnp.concatenate([up_rest, down_rest], axis=0)
    left_rest, right_rest = shift(rest, 1, 0), shift(rest, -1, 0)
    up2, down2 = shift(up1, 0, 1), shift(down1, 0, -1)
    (p_up1, p_down1), (left_quad, right_quad) = project_next(
        [up1, down1],
        [(0, 0, line(X_ORDER, -1), 0, 0), (1, 0, line(X_ORDER, 1), 1, 0)],
        [line_rows] * 2,
        [],
        [left_quad, right_quad],
    )
    far_quad = shift(left_quad, 1, 0)
    (to_right_head, to_left_head, p_right_head, p_left_head, p_tail), (up2, down2) = project_next(
        [left_quad, right_quad, rest],
        [
            (0, 0, column(-1, QUAD[:2]), 1, pair_rows),
            (0, pair_rows, column(-1, QUAD[2:]), 3, 0),
            (1, 0, column(1, QUAD[:2]), 2, 0),
            (1, pair_rows, column(1, QUAD[2:]), 0, pair_rows),
            (2, 0, column(0, REST), 4, 0),
        ],
        [quad_rows, quad_rows, pair_rows, pair_rows, quad_rows],
        [],
        [up2, down2],
    )
    up3, down3 = shift(up2, 0, 1), shift(down2, 0, -1)
    (p_up2, p_down2), (left_rest, right_rest) = project_next(
        [up2, down2],
        [(0, 0, line(X_ORDER, -2), 0, 0), (1, 0, line(X_ORDER, 2), 1, 0)],
        [line_rows] * 2,
        [],
        [left_rest, right_rest],
    )
    far_rest = shift(right_rest, -1, 0)
    parts, (up3, down3) = project_next(
        [far_quad, left_rest, right_rest],
        [
            (0, 0, column(2, QUAD[:2]), 0, 0),
            (0, pair_rows, column(2, QUAD[2:]), 1, 0),
            (1, 0, column(-1, REST[:2]), 3, pair_rows),
            (1, pair_rows, column(-1, REST[2:]), 5, 0),
            (2, 0, column(1, REST[:2]), 4, 0),
            (2, pair_rows, column(1, REST[2:]), 2, pair_rows),
        ],
        [quad_rows] * 4 + [pair_rows] * 2,
        [to_right_head, to_left_head],
        [up3, down3],
    )
    to_right_head, to_left_head, to_right_tail, to_left_tail, p_right_tail, p_left_tail = parts
    left_head, right_head = shift(to_right_head, 1, 0), shift(to_left_head, -1, 0)
    up4, down4 = shift(up3[: line_rows // 2], 0, 1), shift(down3[line_rows // 2 :], 0, -1)
    (to_right_tail, to_left_tail, p_up3, p_down3), (up4, down4) = project_next(
        [far_rest, up3, down3],
        [
            (0, 0, column(2, REST[:2]), 0, 0),
            (0, pair_rows, column(2, REST[2:]), 1, 0),
            (1, 0, line(X_ORDER, -3), 2, 0),
            (2, 0, line(X_ORDER, 3), 3, 0),
        ],
        [quad_rows, quad_rows, line_rows, line_rows],
        [to_right_tail, to_left_tail],
        [up4, down4],
    )
    left_tail, right_tail = shift(to_right_tail, 1, 0), shift(to_left_tail, -1, 0)
    (p_up4, p_down4), _ = project_next(
        [up4, down4],
        [(0, 0, line(X_ORDER[:2], 4), 0, 0), (1, 0, line(X_ORDER[2:], 4), 1, 0)],
        [line_rows // 2] * 2,
        [],
        [],
    )
    top, bottom = shift(p_up4, 0, -1), shift(p_down4, 0, 1)

    order = Order()
    cut = line_rows // 2
    left_head, right_head = order.done(left_head, right_head)
    p_up3, p_down3 = order.tie(p_up3, p_down3)
    p_up3 = jnp.concatenate([add(p_up3[:cut], top), p_up3[cut:]], axis=0)
    p_down3 = jnp.concatenate([p_down3[:cut], add(p_down3[cut:], bottom)], axis=0)
    p_up3, p_down3 = order.done(p_up3, p_down3)
    top, bottom = shift(p_up3, 0, -1), shift(p_down3, 0, 1)
    stream = send_hidden(order)
    p_up2, p_down2 = order.tie(p_up2, p_down2)
    p_up2, p_down2 = order.done(add(p_up2, top), add(p_down2, bottom))
    top, bottom = shift(p_up2, 0, -1), shift(p_down2, 0, 1)
    p_right_tail, p_left_tail = order.tie(p_right_tail, p_left_tail)
    to_right = [add(p_right_tail, left_tail[:pair_rows]), add(p_right_head, left_head[:pair_rows])]
    to_left = [add(p_left_tail, right_tail[:pair_rows]), add(p_left_head, right_head[:pair_rows])]
    to_right, to_left = order.done(
        jnp.concatenate(to_right, axis=0), jnp.concatenate(to_left, axis=0)
    )
    passed_right, passed_left = shift(to_right, 1, 0), shift(to_left, -1, 0)
    p_up1, p_down1 = order.tie(p_up1, p_down1)
    p_up1, p_down1 = order.done(add(p_up1, top), add(p_down1, bottom))
    top, bottom = shift(p_up1, 0, -1), shift(p_down1, 0, 1)
    p_tail = order.tie(p_tail)
    upper, lower = order.done(
        add(p_tail[:pair_rows], right_tail[pair_rows:], passed_right[:pair_rows]),
        add(p_tail[pair_rows:], left_tail[pair_rows:], passed_left[:pair_rows]),
    )
    from_above, from_below = shift(upper, 0, -1), shift(lower, 0, 1)
    p_row = order.tie(p_row)
    row = order.done(add(p_row, top, bottom))
    share = SHARES[1]
    terms = [
        row[:share],
        shift(row[share : 2 * share], -1, 0),
        shift(row[2 * share : 3 * share], 1, 0),
        shift(row[3 * share :], 2, 0),
    ]
    p_head, stream = order.tie(p_head, stream)
    p_head = order.done(
        jnp.concatenate(
            [
                add(p_head[:pair_rows], right_head[pair_rows:], passed_right[pair_rows:]),
                add(p_head[pair_rows:], left_head[pair_rows:], passed_left[pair_rows:]),
            ],
            axis=0,
        )
    )
    share = SHARES[0]
    behind = add(p_head[share : 2 * share], from_above[:share])
    opposite = add(p_head[2 * share : 3 * share], from_above[share:], from_below[:share])
    ahead = add(p_head[3 * share :], from_below[share:])
    others = [shift(opposite, 0, 4), p_head[:share], shift(behind, 0, -1), shift(ahead, 0, 1)]
    others, stream = lax.optimization_barrier((others, in_hbm(stream)))
    first = sum(term.astype(jnp.float32) for term in others)
    second = sum(term.astype(jnp.float32) for term in terms)
    return jnp.concatenate([first, second], axis=0), stream


def body(projected, positions, out_weight, residual, norm_gain, next_weight):
    local_rows = projected[0]
    outer = lax.axis_index("outer")
    inner = lax.axis_index("inner")
    here = jnp.stack([outer % NX, inner * 2 + outer // NX])

    def send_weight(quad):
        quad, weight = lax.optimization_barrier((quad, next_weight[0]))
        scaled = weight.astype(jnp.float32) * norm_gain[0].astype(jnp.float32)[:, None]
        return quad, section_shift(scaled.astype(jnp.bfloat16), -1)

    (first, second), weight_next = attention(
        here, positions[::SUB], local_rows, send_weight
    )
    hidden = []

    def project_next(chunks, pieces, part_rows, started, held):
        outs, parts = project(
            here,
            (out_weight[0], weight_next),
            residual[0],
            hidden,
            chunks,
            pieces,
            part_rows,
            started,
        )
        if held:
            outs[0], held = lax.optimization_barrier((outs[0], held))
        hidden[:] = outs
        return parts, held

    def send_hidden(order):
        return section_shift(order.tie(hidden[0])[None], 1)

    summed, stream = exchange(first, second, project_next, send_hidden)
    inverse_rms = lax.rsqrt(summed[:, QW : QW + 1] / D + 1e-05)
    result = (summed[:, :QW] * inverse_rms).astype(jnp.bfloat16)
    return (section_shift(result[None], 1), stream)


def solution(mesh):
    return jax.shard_map(
        body,
        mesh=mesh,
        in_specs=(
            P("section", ("outer", "inner"), None),
            P(),
            P("section", None, ("outer", "inner")),
            P("section", None, ("outer", "inner")),
            P("section", ("outer", "inner")),
            P("section", ("outer", "inner"), None),
        ),
        out_specs=(P("section", ("outer", "inner"), None), P("section", None, ("outer", "inner"))),
        check_vma=False,
    )
```
